256 devices in a mesh: dp: 64 (over x, z_lo, y, core), mp: 4 (over z_hi).
Axes of the slice: x: 4, y: 4, z: 8 (z_hi: 4, z_lo: 2; z = z_hi * 2 + z_lo), core: 2. Of those that a mesh axis runs over, the one named last changes fastest.
Arguments:
- train_acts: bfloat16 [32768, 2560], P('dp'), may hold values from -6 to 6
- train_grads: bfloat16 [32768, 2560], P('dp'), may hold values from -6 to 6
- lengths: int32 [256], P('dp'), may hold values from 1 to 256, as said below
- query_acts: bfloat16 [128, 2560], replicated, may hold values from -6 to 6
- query_grads: bfloat16 [128, 2560], replicated, may hold values from -0.0059814453 to 0.0059814453
- basis_in: bfloat16 [2560, 2560], P(None, 'mp'), may hold values from -0.125 to 0.125
- basis_out: bfloat16 [2560, 2560], P(None, 'mp'), may hold values from -0.125 to 0.125
Outputs:
- scores: float32 [1, 256], P(None, 'dp')
The draws below stay inside these ranges and needn't reach their ends.
Inputs may be any that keep to these rules, and one draw needn't show every extreme that they name: The 4 lengths of one index of dp sum to at most 512; in every draw some index's sequences fill all 512 rows and one of them has exactly 256 tokens.
All inputs are finite; a program needn't handle non-finite values.
Results may differ from the reference program's by a relative error of at most 0.0045.
Values may be sent and summed in bfloat16 or wider, within the bound.
No kernel may reach another device: no remote copies, remote signals or barrier semaphores. Data moves between devices by JAX's collectives and lax.ppermute only.
A program may use at most 128 MiB of HBM per device.

```python
import jax
import jax.numpy as jnp
from jax import lax

D_IN = 2560
D_OUT = 2560
TOK_CAP = 512
SEQ_DEV = 4
QUERIES = 1
QLEN = 128
SEQ_MAX = 256
TOKENS = 32768
SEQUENCES = 256


def draw_lengths(key, part):
    groups = SEQUENCES // SEQ_DEV
    key_total = jax.random.fold_in(key, 11)
    key_weight = jax.random.fold_in(key, 12)
    key_device = jax.random.fold_in(key, 13)
    key_slot = jax.random.fold_in(key, 14)
    totals = jax.random.randint(key_total, (groups,), TOK_CAP // 4, TOK_CAP - TOK_CAP // 8 + 1)
    weights = jax.random.randint(key_weight, (groups, SEQ_DEV), 1, 3)
    cumulative = jnp.cumsum(weights, axis=1)
    whole = cumulative[:, -1:]
    bounds = totals[:, None] * cumulative // whole
    previous = jnp.concatenate([jnp.zeros((groups, 1), jnp.int32), bounds[:, :-1]], axis=1)
    general = bounds - previous
    full_device = jax.random.randint(key_device, (), 0, groups)
    full_slot = jax.random.randint(key_slot, (), 0, SEQ_DEV)
    slots = jnp.arange(SEQ_DEV, dtype=jnp.int32)
    full_weights = jnp.where(slots == full_slot, 0, weights[full_device])
    full_cumulative = jnp.cumsum(full_weights)
    remainder = TOK_CAP - SEQ_MAX
    full_bounds = remainder * full_cumulative // full_cumulative[-1]
    full_previous = jnp.concatenate([jnp.zeros((1,), jnp.int32), full_bounds[:-1]])
    full_lengths = jnp.where(slots == full_slot, SEQ_MAX, full_bounds - full_previous)
    rows = jnp.arange(groups, dtype=jnp.int32)
    result = jnp.where((rows == full_device)[:, None], full_lengths[None, :], general)
    return result.reshape(SEQUENCES).astype(jnp.int32)


def level_of(stream_key, dims, split, low, top_value):
    loudness = 1.0
    for axis_at, shards_of in split:
        steps = jax.random.uniform(jax.random.fold_in(jax.random.fold_in(stream_key, 6), axis_at), (shards_of,), jnp.float32, low / len(split), top_value / len(split))
        loudness = loudness * jnp.repeat(jnp.exp(steps), dims[axis_at] // shards_of).reshape((-1,) + (1,) * (len(dims) - 1 - axis_at))
    return loudness


def scatter_about(key, shape, deviation, most, split=(), kind=jnp.bfloat16):
    drawn = deviation * jax.random.normal(key, shape, jnp.float32)
    if split:
        drawn = drawn * level_of(key, shape, split, -0.22, 0.18)
    return jnp.clip(drawn, -most, most).astype(kind)


def setup_inputs(seed: int = 0) -> dict:
    streams_of = jax.random.split(jax.random.key(seed), 8)
    return {
        "train_acts": scatter_about(streams_of[0], (TOKENS, D_IN), 1.0, 6.0, ((0, 64),)),
        "train_grads": scatter_about(streams_of[1], (TOKENS, D_OUT), 1.0, 6.0, ((0, 64),)),
        "lengths": draw_lengths(jax.random.fold_in(streams_of[7], 71), 0),
        "query_acts": scatter_about(streams_of[3], (QUERIES * QLEN, D_IN), 1.0, 6.0),
        "query_grads": scatter_about(streams_of[4], (QUERIES * QLEN, D_OUT), 0.001, 0.0059814453),
        "basis_in": scatter_about(streams_of[5], (D_IN, D_IN), D_IN ** -0.5, 0.125, ((1, 4),)),
        "basis_out": scatter_about(streams_of[6], (D_OUT, D_OUT), D_OUT ** -0.5, 0.125, ((1, 4),)),
    }


damping_ratio = 0.1

def rotate(values, basis):
    return jnp.dot(values, basis, preferred_element_type=jnp.float32).astype(jnp.bfloat16)

def reference(train_acts, train_grads, lengths, query_acts, query_grads, basis_in, basis_out):
    groups = SEQUENCES // SEQ_DEV
    acts_rot = rotate(train_acts, basis_in).reshape(groups, TOK_CAP, D_IN)
    grads_rot = rotate(train_grads, basis_out).reshape(groups, TOK_CAP, D_OUT)
    seq_lengths = lengths.reshape(groups, SEQ_DEV).astype(jnp.int32)
    finish = jnp.cumsum(seq_lengths, axis=1).astype(jnp.int32)
    starts = (finish - seq_lengths).astype(jnp.int32)
    position = jnp.arange(SEQ_MAX, dtype=jnp.int32)

    def sequence_grad(index):
        device = (index // SEQ_DEV).astype(jnp.int32)
        slot = (index % SEQ_DEV).astype(jnp.int32)
        first = starts[device, slot]
        last = finish[device, slot]
        begin = jnp.minimum(first, TOK_CAP - SEQ_MAX).astype(jnp.int32)
        grads_win = lax.dynamic_slice_in_dim(grads_rot[device], begin, SEQ_MAX, 0)
        acts_win = lax.dynamic_slice_in_dim(acts_rot[device], begin, SEQ_MAX, 0)
        inside = (position + begin >= first) & (position + begin < last)
        grads_win = jnp.where(inside[:, None], grads_win, jnp.zeros_like(grads_win))
        return jnp.dot(grads_win.T.astype(jnp.float32), acts_win.astype(jnp.float32), preferred_element_type=jnp.float32)

    def add_square(index, running):
        product = sequence_grad(index)
        return running + product * product
    curvature = lax.fori_loop(0, SEQUENCES, add_square, jnp.zeros((D_OUT, D_IN), jnp.float32)) / SEQUENCES
    damping = damping_ratio * jnp.mean(curvature)
    query_g = rotate(query_grads, basis_out).astype(jnp.float32).reshape(QUERIES, QLEN, D_OUT)
    query_a = rotate(query_acts, basis_in).astype(jnp.float32).reshape(QUERIES, QLEN, D_IN)
    query_grad = jnp.einsum('qti,qtj->qij', query_g, query_a)
    precond = (query_grad / (curvature + damping)).astype(jnp.bfloat16)
    precond = lax.optimization_barrier(precond).astype(jnp.float32)

    def score_column(index):
        stored = sequence_grad(index).astype(jnp.bfloat16)
        stored = lax.optimization_barrier(stored).astype(jnp.float32)
        return jnp.einsum('qij,ij->q', precond, stored)
    columns = lax.map(score_column, jnp.arange(SEQUENCES, dtype=jnp.int32))
    return columns.T
```

```python
import functools

import jax
import jax.numpy as jnp
import numpy as np
from jax import lax
from jax.experimental import pallas as pl
from jax.experimental.pallas import tpu as pltpu
from jax.sharding import Mesh
from jax.sharding import PartitionSpec as P

DAMPING_RATIO = 0.1
DP = ("x", "zl", "y", "c")
RING = ("x", "zl", "y")
BLOCKS = ("c", "m")
HALF = 256
VMEM = 60 * 1024 * 1024
f32 = jnp.float32
bf16 = jnp.bfloat16


def params():
    return pltpu.CompilerParams(vmem_limit_bytes=VMEM)


def dot(a, b, contract):
    return lax.dot_general(a, b, (contract, ((), ())), preferred_element_type=f32)


def rotate_kernel(transposed, tokens_ref, query_ref, basis_ref, *rest):
    outs, acc = rest[:-1], rest[-1]
    k = pl.program_id(0)
    rows = tokens_ref.shape[0]

    @pl.when(k == 0)
    def _():
        acc[...] = jnp.zeros_like(acc)

    basis = basis_ref[...]
    acc[:rows] += dot(tokens_ref[...], basis, ((1,), (0,)))
    acc[rows:] += dot(query_ref[...], basis, ((1,), (0,)))

    @pl.when(k == pl.num_programs(0) - 1)
    def _():
        if transposed:
            outs[0][...] = acc[:rows].T.astype(bf16)
            outs[1][...] = acc[rows:].T.astype(bf16)
        else:
            outs[0][...] = acc[...].astype(bf16)


def rotate(tokens, query, basis, transposed):
    rows, depth = tokens.shape
    qrows, width = query.shape[0], basis.shape[1]
    step = 512
    if transposed:
        shapes = [(width, rows), (width, qrows)]
    else:
        shapes = [(rows + qrows, width)]
    return pl.pallas_call(
        functools.partial(rotate_kernel, transposed),
        grid=(depth // step,),
        in_specs=[
            pl.BlockSpec((rows, step), lambda k: (0, k)),
            pl.BlockSpec((qrows, step), lambda k: (0, k)),
            pl.BlockSpec((step, width), lambda k: (k, 0)),
        ],
        out_specs=[pl.BlockSpec(s, lambda k: (0, 0)) for s in shapes],
        out_shape=[jax.ShapeDtypeStruct(s, bf16) for s in shapes],
        scratch_shapes=[pltpu.VMEM((rows + qrows, width), f32)],
        compiler_params=params(),
    )(tokens, query, basis)


def bounds_of(lengths_ref, which):
    result, at = [], jnp.int32(0)
    for j in range(lengths_ref.shape[1]):
        end = at + lengths_ref[which, j]
        result.append((at, end))
        at = end
    return result


def curvature_kernel(
    lengths_ref, g00, g01, g10, g11, a0_ref, a1_ref, out_ref, total_ref, masked, wide, g_ref, acc
):
    i = pl.program_id(0)
    first_member = i < pl.num_programs(0) // 2
    acts = (a0_ref, a1_ref)
    tokens = a0_ref.shape[0]
    count = lengths_ref.shape[1]

    @pl.when(i == 0)
    def _():
        total_ref[...] = jnp.zeros_like(total_ref)
        row = lax.broadcasted_iota(jnp.int32, (HALF, 1), 0)
        rows = lax.broadcasted_iota(jnp.int32, (tokens, 1), 0)
        for b in range(2):
            for j, (start, finish) in enumerate(bounds_of(lengths_ref, b)):
                base = jnp.where(start >= HALF, HALF, 0)
                at = pl.multiple_of(base, HALF)
                inside = (row + base >= start) & (row + base < finish)
                window = acts[b][pl.ds(at, HALF), :]
                masked[b * count + j] = jnp.where(inside, window, jnp.zeros_like(window))

                @pl.when((start < HALF) & (finish > HALF))
                def _(b=b, start=start, finish=finish):
                    inside = (rows >= start) & (rows < finish)
                    window = acts[b][0:tokens, :]
                    wide[b] = jnp.where(inside, window, jnp.zeros_like(window))

    g_ref[0] = jnp.where(first_member, g00[...], g10[...])
    g_ref[1] = jnp.where(first_member, g01[...], g11[...])
    for b in range(2):
        for j, (start, finish) in enumerate(bounds_of(lengths_ref, b)):
            at = pl.multiple_of(jnp.where(start >= HALF, HALF, 0), HALF)
            across = (start < HALF) & (finish > HALF)
            opening = b == 0 and j == 0

            def add(product, opening=opening):
                if opening:
                    acc[...] = product * product
                else:
                    acc[...] += product * product

            @pl.when(jnp.logical_not(across))
            def _(b=b, j=j, at=at, add=add):
                add(dot(g_ref[b, :, pl.ds(at, HALF)], masked[b * count + j], ((1,), (0,))))

            @pl.when(across)
            def _(b=b, add=add):
                add(dot(g_ref[b], wide[b], ((1,), (0,))))

    total = acc[...]
    out_ref[...] = total.astype(bf16)
    total_ref[...] += jnp.sum(total, axis=0, keepdims=True)


def curvature_of(lengths, g00, g01, g10, g11, a0, a1):
    width, tokens = g00.shape
    cols = a0.shape[1]
    tile = width // 2
    count = lengths.shape[1]
    near = pl.BlockSpec((tile, tokens), lambda i, *_: (jnp.minimum(i, 1), 0))
    far = pl.BlockSpec((tile, tokens), lambda i, *_: (jnp.maximum(i - 2, 0), 0))
    acts = pl.BlockSpec((tokens, cols), lambda i, *_: (0, 0))
    return pl.pallas_call(
        curvature_kernel,
        grid_spec=pltpu.PrefetchScalarGridSpec(
            num_scalar_prefetch=1,
            grid=(4,),
            in_specs=[near, near, far, far, acts, acts],
            out_specs=[
                pl.BlockSpec((tile, cols), lambda i, *_: (i, 0)),
                pl.BlockSpec((1, cols), lambda i, *_: (0, 0)),
            ],
            scratch_shapes=[
                pltpu.VMEM((2 * count, HALF, cols), bf16),
                pltpu.VMEM((2, tokens, cols), bf16),
                pltpu.VMEM((2, tile, tokens), bf16),
                pltpu.VMEM((tile, cols), f32),
            ],
        ),
        out_shape=[
            jax.ShapeDtypeStruct((2 * width, cols), bf16),
            jax.ShapeDtypeStruct((1, cols), f32),
        ],
        compiler_params=params(),
    )(lengths, g00, g01, g10, g11, a0, a1)


def precond_kernel(scale, damping_ref, parts_ref, qg_ref, qa_ref, out_ref):
    total = parts_ref[0].astype(f32)
    for j in range(1, parts_ref.shape[0]):
        total = total + parts_ref[j].astype(f32)
    query = dot(qg_ref[...], qa_ref[...], ((1,), (0,)))
    value = (query / (total * scale + damping_ref[0, 0])).astype(bf16)
    for j in range(out_ref.shape[0]):
        out_ref[j] = value


def precond_of(scale, damping, parts, qg, qa):
    return pl.pallas_call(
        functools.partial(precond_kernel, scale),
        in_specs=[pl.BlockSpec(memory_space=pltpu.SMEM)] + [pl.BlockSpec(memory_space=pltpu.VMEM)] * 3,
        out_specs=pl.BlockSpec(memory_space=pltpu.VMEM),
        out_shape=jax.ShapeDtypeStruct(parts.shape, bf16),
        compiler_params=params(),
    )(damping, parts, qg, qa)


def score_kernel(lengths_ref, p_ref, g00, g01, g10, g11, a0_ref, a1_ref, out_ref, sums):
    i = pl.program_id(0)
    first_member = i < pl.num_programs(0) // 2
    tokens = g00.shape[1]

    @pl.when(i == 0)
    def _():
        sums[...] = jnp.zeros_like(sums)

    precond = p_ref[...]
    for b, (near, far, acts) in enumerate(((g00, g10, a0_ref), (g01, g11, a1_ref))):
        grads = jnp.where(first_member, near[...], far[...]).astype(f32)
        moved = dot(precond, acts[0:tokens, :], ((1,), (1,)))
        sums[b : b + 1] += jnp.sum(grads * moved, axis=0, keepdims=True)

    @pl.when(i == pl.num_programs(0) - 1)
    def _():
        lane = lax.broadcasted_iota(jnp.int32, (1, tokens), 1)
        for b in range(2):
            for j, (start, finish) in enumerate(bounds_of(lengths_ref, b)):
                inside = (lane >= start) & (lane < finish)
                value = jnp.sum(jnp.where(inside, sums[b : b + 1], 0.0), axis=1, keepdims=True)
                out_ref[b, j : j + 1, :] = jnp.broadcast_to(value, (1, out_ref.shape[2]))


def scores_of(lengths, precond, g00, g01, g10, g11, a0, a1):
    width, tokens = g00.shape
    cols = a0.shape[1]
    tile = width // 2
    count = lengths.shape[1]
    near = pl.BlockSpec((tile, tokens), lambda i, *_: (jnp.minimum(i, 1), 0))
    far = pl.BlockSpec((tile, tokens), lambda i, *_: (jnp.maximum(i - 2, 0), 0))
    acts = pl.BlockSpec((tokens, cols), lambda i, *_: (0, 0))
    return pl.pallas_call(
        score_kernel,
        grid_spec=pltpu.PrefetchScalarGridSpec(
            num_scalar_prefetch=1,
            grid=(4,),
            in_specs=[
                pl.BlockSpec((tile, cols), lambda i, *_: (i, 0)),
                near, near, far, far, acts, acts,
            ],
            out_specs=pl.BlockSpec((2, count, 128), lambda i, *_: (0, 0, 0)),
            scratch_shapes=[pltpu.VMEM((2, tokens), f32)],
        ),
        out_shape=jax.ShapeDtypeStruct((2, count, 128), f32),
        compiler_params=params(),
    )(lengths, precond, g00, g01, g10, g11, a0, a1)


def routes(f):
    return [(c * 4 + m, f(c, m)[0] * 4 + f(c, m)[1]) for c in range(2) for m in range(4)]


OTHER_CORE = routes(lambda c, m: (1 - c, m))
GRADS_PARTNER = routes(lambda c, m: (c, m ^ 1))
ACTS_SAME = routes(lambda c, m: (0, m) if c == 0 else (1, 3 - m))
ACTS_OTHER = routes(lambda c, m: (0, m) if c == 1 else (1, 3 - m))


def sent_to_all(array, axes, count):
    return lax.all_to_all(jnp.broadcast_to(array[None], (count, *array.shape)), axes, 0, 0, tiled=True)


def shards(train_acts, train_grads, lengths, query_acts, query_grads, basis_in, basis_out):
    core = lax.axis_index("c")
    ring = lax.axis_index(RING)
    ring_size = lax.axis_size(RING)
    tokens = train_acts.shape[0]
    count = lengths.shape[0]

    g00, qg_own = rotate(train_grads, query_grads, basis_out, True)
    both = jnp.stack([lengths, lax.ppermute(lengths, BLOCKS, OTHER_CORE)])
    g10 = lax.ppermute(g00, BLOCKS, GRADS_PARTNER)
    g01 = lax.ppermute(g00, BLOCKS, OTHER_CORE)
    (acts,) = rotate(train_acts, query_acts, basis_in, False)
    a1 = lax.ppermute(acts, BLOCKS, ACTS_OTHER)
    a0 = lax.ppermute(acts[:tokens], BLOCKS, ACTS_SAME)
    g11 = lax.ppermute(g10, BLOCKS, OTHER_CORE)
    qa = a1[tokens:]
    a1 = a1[:tokens]

    width, cols = g00.shape[0], a0.shape[1]
    chunk = 2 * width // ring_size
    inner = ring_size // 2
    qg_mine = lax.dynamic_slice_in_dim(qg_own, lax.rem(ring, inner) * chunk, chunk, 0)
    qg_far = lax.ppermute(qg_mine, BLOCKS, GRADS_PARTNER)
    qg = jnp.where(ring < inner, qg_mine, qg_far)

    curvature, totals = curvature_of(both, g00, g01, g10, g11, a0, a1)
    parts = lax.all_to_all(curvature.reshape(ring_size, chunk, cols), RING, 0, 0, tiled=True)
    total = jnp.sum(totals).reshape(1, 1)
    total = jnp.sum(sent_to_all(total, RING, ring_size), axis=0)
    total = jnp.sum(sent_to_all(total, BLOCKS, 8), axis=0)
    scale = 1.0 / (count * lax.axis_size(DP))
    entries = 2 * width * cols * 8
    damping = total * (DAMPING_RATIO * scale / entries)

    mine = precond_of(scale, damping, parts, qg, qa)
    precond = lax.all_to_all(mine, RING, 0, 0, tiled=True).reshape(2 * width, cols)
    found = scores_of(both, precond, g00, g01, g10, g11, a0, a1)[:, :, 0]
    by_core = jnp.where(core == 0, found, found[::-1])
    sent = jnp.broadcast_to(by_core[:, None], (2, 4, count)).reshape(8, 1, count)
    return jnp.sum(lax.all_to_all(sent, BLOCKS, 0, 0, tiled=True), axis=0)


def solution(mesh):
    cut = Mesh(np.asarray(mesh.devices).reshape(4, 2, 4, 2, 4), ("x", "zl", "y", "c", "m"))
    return jax.shard_map(
        shards,
        mesh=cut,
        in_specs=(P(DP, None), P(DP, None), P(DP), P(), P(), P(None, "m"), P(None, "m")),
        out_specs=P(None, DP),
        check_vma=False,
    )
```

```python
import functools

import jax
import jax.numpy as jnp
import numpy as np
from jax import lax
from jax.experimental import pallas as pl
from jax.experimental.pallas import tpu as pltpu
from jax.sharding import Mesh
from jax.sharding import PartitionSpec as P

DAMPING_RATIO = 0.1
DP = ("x", "zl", "y", "c")
RING = ("x", "zl", "y")
BLOCKS = ("c", "m")
HALF = 256
VMEM = 24 * 1024 * 1024
f32 = jnp.float32
bf16 = jnp.bfloat16


def params():
    return pltpu.CompilerParams(vmem_limit_bytes=VMEM)


def dot(a, b, contract):
    return lax.dot_general(a, b, (contract, ((), ())), preferred_element_type=f32)


def rotate(values, basis):
    return dot(values, basis, ((1,), (0,))).astype(bf16)


def rotate_transposed(values, basis):
    return dot(basis, values, ((0,), (1,))).astype(bf16)


def in_vmem(*arrays):
    return [pltpu.with_memory_space_constraint(a, pltpu.VMEM) for a in arrays]


def local_call(kernel, shapes, scratch=(), scalars=1):
    def call(*operands):
        here = pl.BlockSpec(memory_space=pltpu.VMEM)
        there = pl.BlockSpec(memory_space=pltpu.SMEM)
        return pl.pallas_call(
            kernel,
            in_specs=[there] * scalars + [here] * (len(operands) - scalars),
            out_specs=[here] * len(shapes),
            out_shape=list(shapes),
            scratch_shapes=list(scratch),
            compiler_params=params(),
        )(*operands[:scalars], *in_vmem(*operands[scalars:]))

    return call


def bounds_of(lengths_ref, which):
    result, at = [], jnp.int32(0)
    for j in range(lengths_ref.shape[1]):
        end = at + lengths_ref[which, j]
        result.append((at, end))
        at = end
    return result


def pick(index, values):
    chosen = values[0]
    for j in range(1, len(values)):
        chosen = jnp.where(index == j, values[j], chosen)
    return chosen


def curvature_kernel(rt, lengths_ref, g00, g01, g10, g11, a0_ref, a1_ref, out_ref, masked, wide):
    acts = (a0_ref, a1_ref)
    tokens, cols = a0_ref.shape
    width = g00.shape[0]
    count = lengths_ref.shape[1]
    row = lax.broadcasted_iota(jnp.int32, (HALF, 1), 0)
    rows = lax.broadcasted_iota(jnp.int32, (tokens, 1), 0)
    places = []
    for b in range(2):
        bounds = bounds_of(lengths_ref, b)
        starts, ends = [v[0] for v in bounds], [v[1] for v in bounds]
        across = jnp.int32(count - 1)
        for j, (start, finish) in enumerate(bounds):
            across = jnp.where((start < HALF) & (finish > HALF), j, across)
        inside = (rows >= pick(across, starts)) & (rows < pick(across, ends))
        wide[b] = jnp.where(inside, acts[b][...], jnp.zeros((tokens, cols), bf16))
        for k in range(count - 1):
            which = k + (k >= across).astype(jnp.int32)
            start, finish = pick(which, starts), pick(which, ends)
            base = jnp.where(start >= HALF, HALF, 0)
            at = pl.multiple_of(base, HALF)
            inside = (row + base >= start) & (row + base < finish)
            window = acts[b][pl.ds(at, HALF), :]
            masked[b * (count - 1) + k] = jnp.where(inside, window, jnp.zeros_like(window))
            places.append((b, b * (count - 1) + k, at))

    sums = jnp.zeros((1, cols), f32)
    for member, grads in enumerate(((g00, g01), (g10, g11))):

        def body(i, sums, member=member, grads=grads):
            r = pl.multiple_of(i * rt, rt)
            total = None
            for b in range(2):
                product = dot(grads[b][pl.ds(r, rt), :], wide[b], ((1,), (0,)))
                total = product * product if total is None else total + product * product
            for b, slot, at in places:
                product = dot(grads[b][pl.ds(r, rt), pl.ds(at, HALF)], masked[slot], ((1,), (0,)))
                total = total + product * product
            out_ref[pl.ds(member * width + r, rt), 0:cols] = total.astype(bf16)
            return sums + jnp.sum(total, axis=0, keepdims=True)

        sums = lax.fori_loop(0, width // rt, body, sums)
    total = jnp.sum(sums, axis=1, keepdims=True)
    high = total.astype(bf16)
    rest = total - high.astype(f32)
    middle = rest.astype(bf16)
    low = (rest - middle.astype(f32)).astype(bf16)
    lane = lax.broadcasted_iota(jnp.int32, (1, 128), 1)
    terms = jnp.where(lane == 0, high.astype(f32), jnp.where(lane == 1, middle.astype(f32), low.astype(f32)))
    terms = jnp.where(lane < 3, terms, 0.0)
    out_ref[:, cols:] = jnp.broadcast_to(terms, (out_ref.shape[0], 128)).astype(bf16)


def curvature_of(lengths, g00, g01, g10, g11, a0, a1):
    width = g00.shape[0]
    tokens, cols = a0.shape
    count = lengths.shape[1]
    return local_call(
        functools.partial(curvature_kernel, width),
        [jax.ShapeDtypeStruct((2 * width, cols + 128), bf16)],
        [pltpu.VMEM((2 * (count - 1), HALF, cols), bf16), pltpu.VMEM((2, tokens, cols), bf16)],
    )(lengths, g00, g01, g10, g11, a0, a1)[0]


def precond_kernel(scale, damping_ref, parts_ref, qg_ref, qa_ref, out_ref):
    cols = qa_ref.shape[1]
    total = parts_ref[0, :, 0:cols].astype(f32)
    for j in range(1, parts_ref.shape[0]):
        total = total + parts_ref[j, :, 0:cols].astype(f32)
    query = dot(qg_ref[...], qa_ref[...], ((1,), (0,)))
    value = (query / (total * scale + damping_ref[0, 0])).astype(bf16)
    for j in range(out_ref.shape[0]):
        out_ref[j] = value


def precond_of(scale, damping, parts, qg, qa):
    shape = (parts.shape[0], parts.shape[1], qa.shape[1])
    return local_call(
        functools.partial(precond_kernel, scale), [jax.ShapeDtypeStruct(shape, bf16)]
    )(damping, parts, qg, qa)[0]


def score_kernel(lengths_ref, p_ref, g00, g01, g10, g11, a0_ref, a1_ref, out_ref):
    width, tokens = g00.shape
    lane = lax.broadcasted_iota(jnp.int32, (1, tokens), 1)
    for b, (near, far, acts) in enumerate(((g00, g10, a0_ref), (g01, g11, a1_ref))):
        sums = jnp.zeros((1, tokens), f32)
        for member, grads in enumerate((near, far)):
            moved = dot(p_ref[member * width : (member + 1) * width, :], acts[...], ((1,), (1,)))
            sums = sums + jnp.sum(grads[...].astype(f32) * moved, axis=0, keepdims=True)
        for j, (start, finish) in enumerate(bounds_of(lengths_ref, b)):
            inside = (lane >= start) & (lane < finish)
            value = jnp.sum(jnp.where(inside, sums, 0.0), axis=1, keepdims=True)
            out_ref[b, j : j + 1, :] = jnp.broadcast_to(value, (1, out_ref.shape[2]))


def scores_of(lengths, precond, g00, g01, g10, g11, a0, a1):
    return local_call(
        score_kernel, [jax.ShapeDtypeStruct((2, lengths.shape[1], 128), f32)]
    )(lengths, precond, g00, g01, g10, g11, a0, a1)[0]


def routes(f):
    return [(c * 4 + m, f(c, m)[0] * 4 + f(c, m)[1]) for c in range(2) for m in range(4)]


OTHER_CORE = routes(lambda c, m: (1 - c, m))
GRADS_PARTNER = routes(lambda c, m: (c, m ^ 1))
ACTS_PARTNER = routes(lambda c, m: (c, 3 - m))
ACTS_SAME = routes(lambda c, m: (0, m) if c == 0 else (1, 3 - m))
ACTS_OTHER = routes(lambda c, m: (0, m) if c == 1 else (1, 3 - m))


def moved(array, pairs):
    return lax.ppermute(array, BLOCKS, pairs)


def over_partners(value):
    value = value + moved(value, GRADS_PARTNER)
    return value + moved(value, ACTS_PARTNER)


def shards(train_acts, train_grads, lengths, query_acts, query_grads, basis_in, basis_out):
    ring = lax.axis_index(RING)
    ring_size = lax.axis_size(RING)
    count = lengths.shape[0]

    acts = rotate(train_acts, basis_in)
    acts, train_grads = lax.optimization_barrier((acts, train_grads))
    a1 = moved(acts, ACTS_OTHER)
    a0 = moved(acts, ACTS_SAME)
    g00 = rotate_transposed(train_grads, basis_out)
    g00, query_acts, query_grads = lax.optimization_barrier((g00, query_acts, query_grads))
    g10 = moved(g00, GRADS_PARTNER)
    g01 = moved(g00, OTHER_CORE)
    g11 = moved(g10, OTHER_CORE)
    both = jnp.stack([lengths, moved(lengths, OTHER_CORE)])

    width, cols = g00.shape[0], a0.shape[1]
    chunk = 2 * width // ring_size
    inner = ring_size // 2
    qa = rotate(query_acts, basis_in)
    qg_own = rotate_transposed(query_grads, basis_out)
    qg_mine = lax.dynamic_slice_in_dim(qg_own, lax.rem(ring, inner) * chunk, chunk, 0)
    a1, qa, qg_mine = lax.optimization_barrier((a1, qa, qg_mine))
    qa = moved(qa, ACTS_OTHER)
    qg_far = moved(qg_mine, GRADS_PARTNER)
    qg = jnp.where(ring < inner, qg_mine, qg_far)

    curvature = curvature_of(both, g00, g01, g10, g11, a0, a1)
    parts = lax.all_to_all(curvature.reshape(ring_size, chunk, cols + 128), RING, 0, 0, tiled=True)
    total = jnp.sum(parts[:, 0, cols : cols + 3].astype(f32)).reshape(1, 1)
    total = over_partners(total + moved(total, OTHER_CORE))
    scale = 1.0 / (count * lax.axis_size(DP))
    entries = 2 * width * cols * 8
    damping = total * (DAMPING_RATIO * scale / entries)

    mine = precond_of(scale, damping, parts, qg, qa)
    precond = lax.all_to_all(mine, RING, 0, 0, tiled=True).reshape(2 * width, cols)
    found = scores_of(both, precond, g00, g01, g10, g11, a0, a1)
    found = over_partners(found[0] + moved(found[1], OTHER_CORE))
    return found[:, 0].reshape(1, count)


def solution(mesh):
    cut = Mesh(np.asarray(mesh.devices).reshape(4, 2, 4, 2, 4), ("x", "zl", "y", "c", "m"))
    return jax.shard_map(
        shards,
        mesh=cut,
        in_specs=(P(DP, None), P(DP, None), P(DP), P(), P(), P(None, "m"), P(None, "m")),
        out_specs=P(None, DP),
        check_vma=False,
    )
```

```python
import functools

import jax
import jax.numpy as jnp
import numpy as np
from jax import lax
from jax.experimental import pallas as pl
from jax.experimental.pallas import tpu as pltpu
from jax.sharding import Mesh
from jax.sharding import PartitionSpec as P

DAMPING_RATIO = 0.1
DP = ("x", "zl", "y", "c")
RING = ("x", "zl", "y")
BLOCKS = ("c", "m")
HALF = 256
VMEM = 24 * 1024 * 1024
f32 = jnp.float32
bf16 = jnp.bfloat16


def params():
    return pltpu.CompilerParams(vmem_limit_bytes=VMEM)


def dot(a, b, contract):
    return lax.dot_general(a, b, (contract, ((), ())), preferred_element_type=f32)


def rotate(values, basis):
    return dot(values, basis, ((1,), (0,))).astype(bf16)


def rotate_transposed(values, basis):
    return dot(basis, values, ((0,), (1,))).astype(bf16)


def in_vmem(*arrays):
    return [pltpu.with_memory_space_constraint(a, pltpu.VMEM) for a in arrays]


def local_call(kernel, shapes, scratch=(), scalars=1):
    def call(*operands):
        here = pl.BlockSpec(memory_space=pltpu.VMEM)
        there = pl.BlockSpec(memory_space=pltpu.SMEM)
        return pl.pallas_call(
            kernel,
            in_specs=[there] * scalars + [here] * (len(operands) - scalars),
            out_specs=[here] * len(shapes),
            out_shape=list(shapes),
            scratch_shapes=list(scratch),
            compiler_params=params(),
        )(*operands[:scalars], *in_vmem(*operands[scalars:]))

    return call


def bounds_of(lengths_ref, which):
    result, at = [], jnp.int32(0)
    for j in range(lengths_ref.shape[1]):
        end = at + lengths_ref[which, j]
        result.append((at, end))
        at = end
    return result


def pick(index, values):
    chosen = values[0]
    for j in range(1, len(values)):
        chosen = jnp.where(index == j, values[j], chosen)
    return chosen


def block_curvature(grads, places, masked, wide, finished):
    total = None
    for b in range(2):
        product = dot(grads[b][...], wide[b], ((1,), (0,)))
        total = product * product if total is None else total + product * product
    for b, slot, at in places:
        product = dot(grads[b][:, pl.ds(at, HALF)], masked[slot], ((1,), (0,)))
        total = total + product * product
    finished[...] = total.astype(bf16)
    return jnp.sum(total, axis=0, keepdims=True)


def places_of(lengths_ref):
    count = lengths_ref.shape[1]
    wides, places = [], []
    for b in range(2):
        bounds = bounds_of(lengths_ref, b)
        starts, ends = [v[0] for v in bounds], [v[1] for v in bounds]
        across = jnp.int32(count - 1)
        for j, (start, finish) in enumerate(bounds):
            across = jnp.where((start < HALF) & (finish > HALF), j, across)
        wides.append((pick(across, starts), pick(across, ends)))
        for k in range(count - 1):
            which = k + (k >= across).astype(jnp.int32)
            start = pick(which, starts)
            at = pl.multiple_of(jnp.where(start >= HALF, HALF, 0), HALF)
            places.append((b, b * (count - 1) + k, at, start, pick(which, ends)))
    return wides, places


def near_kernel(lengths_ref, g00, g01, a0_ref, a1_ref, out_hbm, masked, wide, sums_ref, finished, sem):
    acts = (a0_ref, a1_ref)
    tokens, cols = a0_ref.shape
    row = lax.broadcasted_iota(jnp.int32, (HALF, 1), 0)
    rows = lax.broadcasted_iota(jnp.int32, (tokens, 1), 0)
    wides, places = places_of(lengths_ref)
    for b, (start, finish) in enumerate(wides):
        inside = (rows >= start) & (rows < finish)
        wide[b] = jnp.where(inside, acts[b][...], jnp.zeros((tokens, cols), bf16))
    for b, slot, at, start, finish in places:
        inside = (row + at >= start) & (row + at < finish)
        window = acts[b][pl.ds(at, HALF), :]
        masked[slot] = jnp.where(inside, window, jnp.zeros_like(window))
    sums_ref[...] = block_curvature((g00, g01), [p[:3] for p in places], masked, wide, finished)
    width = finished.shape[0]
    copy = pltpu.make_async_copy(finished, out_hbm.at[0:width, 0:cols], sem)
    copy.start()
    copy.wait()


def far_kernel(lengths_ref, _, g10, g11, masked, wide, sums_ref, out_hbm, finished, terms_ref, sems):
    places = places_of(lengths_ref)[1]
    sums = sums_ref[...] + block_curvature((g10, g11), [p[:3] for p in places], masked, wide, finished)
    width, cols = finished.shape
    copy = pltpu.make_async_copy(finished, out_hbm.at[width : 2 * width, 0:cols], sems.at[0])
    copy.start()
    total = jnp.sum(sums, axis=1, keepdims=True)
    high = total.astype(bf16).astype(f32)
    middle = (total - high).astype(bf16).astype(f32)
    low = total - high - middle
    lane = lax.broadcasted_iota(jnp.int32, (1, 128), 1)
    terms = jnp.where(lane == 0, high, jnp.where(lane == 1, middle, jnp.where(lane == 2, low, 0.0)))
    terms_ref[...] = jnp.broadcast_to(terms, terms_ref.shape).astype(bf16)
    also = pltpu.make_async_copy(terms_ref, out_hbm.at[:, cols : cols + 128], sems.at[1])
    also.start()
    copy.wait()
    also.wait()


def near_curvature(lengths, g00, g01, a0, a1):
    width = g00.shape[0]
    tokens, cols = a0.shape
    others = 2 * (lengths.shape[1] - 1)
    here = pl.BlockSpec(memory_space=pltpu.VMEM)
    return pl.pallas_call(
        near_kernel,
        in_specs=[pl.BlockSpec(memory_space=pltpu.SMEM)] + [here] * 4,
        out_specs=[pl.BlockSpec(memory_space=pltpu.HBM), here, here, here],
        out_shape=[
            pltpu.HBM((2 * width, cols + 128), bf16),
            jax.ShapeDtypeStruct((others, HALF, cols), bf16),
            jax.ShapeDtypeStruct((2, tokens, cols), bf16),
            jax.ShapeDtypeStruct((1, cols), f32),
        ],
        scratch_shapes=[pltpu.VMEM((width, cols), bf16), pltpu.SemaphoreType.DMA],
        compiler_params=params(),
    )(lengths, *in_vmem(g00, g01, a0, a1))


def far_curvature(lengths, started, g10, g11, masked, wide, sums):
    width = g10.shape[0]
    cols = sums.shape[1]
    here = pl.BlockSpec(memory_space=pltpu.VMEM)
    anywhere = pl.BlockSpec(memory_space=pltpu.HBM)
    return pl.pallas_call(
        far_kernel,
        in_specs=[pl.BlockSpec(memory_space=pltpu.SMEM), anywhere] + [here] * 5,
        out_specs=anywhere,
        out_shape=pltpu.HBM(started.shape, started.dtype),
        input_output_aliases={1: 0},
        scratch_shapes=[
            pltpu.VMEM((width, cols), bf16),
            pltpu.VMEM((2 * width, 128), bf16),
            pltpu.SemaphoreType.DMA((2,)),
        ],
        compiler_params=params(),
    )(lengths, started, *in_vmem(g10, g11, masked, wide, sums))


def precond_kernel(scale, damping_ref, parts_ref, qg_ref, qa_ref, out_ref):
    cols = qa_ref.shape[1]
    total = parts_ref[0, :, 0:cols].astype(f32)
    for j in range(1, parts_ref.shape[0]):
        total = total + parts_ref[j, :, 0:cols].astype(f32)
    query = dot(qg_ref[...], qa_ref[...], ((1,), (0,)))
    value = (query / (total * scale + damping_ref[0, 0])).astype(bf16)
    for j in range(out_ref.shape[0]):
        out_ref[j] = value


def precond_of(scale, damping, parts, qg, qa):
    shape = (parts.shape[0], parts.shape[1], qa.shape[1])
    return local_call(
        functools.partial(precond_kernel, scale), [jax.ShapeDtypeStruct(shape, bf16)]
    )(damping, parts, qg, qa)[0]


def score_kernel(lengths_ref, p_ref, g00, g01, g10, g11, a0_ref, a1_ref, out_ref):
    width, tokens = g00.shape
    lane = lax.broadcasted_iota(jnp.int32, (1, tokens), 1)
    for b, (near, far, acts) in enumerate(((g00, g10, a0_ref), (g01, g11, a1_ref))):
        sums = jnp.zeros((1, tokens), f32)
        for member, grads in enumerate((near, far)):
            moved = dot(p_ref[member * width : (member + 1) * width, :], acts[...], ((1,), (1,)))
            sums = sums + jnp.sum(grads[...].astype(f32) * moved, axis=0, keepdims=True)
        for j, (start, finish) in enumerate(bounds_of(lengths_ref, b)):
            inside = (lane >= start) & (lane < finish)
            value = jnp.sum(jnp.where(inside, sums, 0.0), axis=1, keepdims=True)
            out_ref[b, j : j + 1, :] = jnp.broadcast_to(value, (1, out_ref.shape[2]))


def scores_of(lengths, precond, g00, g01, g10, g11, a0, a1):
    return local_call(
        score_kernel, [jax.ShapeDtypeStruct((2, lengths.shape[1], 128), f32)]
    )(lengths, precond, g00, g01, g10, g11, a0, a1)[0]


def routes(f):
    return [(c * 4 + m, f(c, m)[0] * 4 + f(c, m)[1]) for c in range(2) for m in range(4)]


OTHER_CORE = routes(lambda c, m: (1 - c, m))
GRADS_PARTNER = routes(lambda c, m: (c, m ^ 1))
ACTS_PARTNER = routes(lambda c, m: (c, 3 - m))
ACTS_SAME = routes(lambda c, m: (0, m) if c == 0 else (1, 3 - m))
ACTS_OTHER = routes(lambda c, m: (0, m) if c == 1 else (1, 3 - m))


def moved(array, pairs):
    return lax.ppermute(array, BLOCKS, pairs)


def over_partners(value):
    value = value + moved(value, GRADS_PARTNER)
    return value + moved(value, ACTS_PARTNER)


def shards(train_acts, train_grads, lengths, query_acts, query_grads, basis_in, basis_out):
    ring = lax.axis_index(RING)
    ring_size = lax.axis_size(RING)
    count = lengths.shape[0]

    acts = rotate(train_acts, basis_in)
    acts, train_grads = lax.optimization_barrier((acts, train_grads))
    a1 = moved(acts, ACTS_OTHER)
    a0 = moved(acts, ACTS_SAME)
    g00 = rotate_transposed(train_grads, basis_out)
    g00, query_acts, query_grads = lax.optimization_barrier((g00, query_acts, query_grads))
    g10 = moved(g00, GRADS_PARTNER)
    g01 = moved(g00, OTHER_CORE)
    both = jnp.stack([lengths, moved(lengths, OTHER_CORE)])

    width, cols = g00.shape[0], a0.shape[1]
    chunk = 2 * width // ring_size
    inner = ring_size // 2
    qa = rotate(query_acts, basis_in)
    qg_own = rotate_transposed(query_grads, basis_out)
    qg_mine = lax.dynamic_slice_in_dim(qg_own, lax.rem(ring, inner) * chunk, chunk, 0)
    g10, qa, qg_mine = lax.optimization_barrier((g10, qa, qg_mine))
    g11 = moved(g10, OTHER_CORE)
    qa = moved(qa, ACTS_OTHER)
    qg_far = moved(qg_mine, GRADS_PARTNER)

    started, masked, wide, sums = near_curvature(both, g00, g01, a0, a1)
    g11, qa, qg_far = lax.optimization_barrier((g11, qa, qg_far))
    qg = jnp.where(ring < inner, qg_mine, qg_far)
    curvature = far_curvature(both, started, g10, g11, masked, wide, sums)
    parts = lax.all_to_all(curvature.reshape(ring_size, chunk, cols + 128), RING, 0, 0, tiled=True)
    total = jnp.sum(parts[:, 0, cols : cols + 3].astype(f32)).reshape(1, 1)
    total = over_partners(total + moved(total, OTHER_CORE))
    scale = 1.0 / (count * lax.axis_size(DP))
    entries = 2 * width * cols * 8
    damping = total * (DAMPING_RATIO * scale / entries)

    mine = precond_of(scale, damping, parts, qg, qa)
    precond = lax.all_to_all(mine, RING, 0, 0, tiled=True).reshape(2 * width, cols)
    found = scores_of(both, precond, g00, g01, g10, g11, a0, a1)
    found = over_partners(found[0] + moved(found[1], OTHER_CORE))
    return found[:, 0].reshape(1, count)


def solution(mesh):
    cut = Mesh(np.asarray(mesh.devices).reshape(4, 2, 4, 2, 4), ("x", "zl", "y", "c", "m"))
    return jax.shard_map(
        shards,
        mesh=cut,
        in_specs=(P(DP, None), P(DP, None), P(DP), P(), P(), P(None, "m"), P(None, "m")),
        out_specs=P(None, DP),
        check_vma=False,
    )
```

```python
import functools

import jax
import jax.numpy as jnp
import numpy as np
from jax import lax
from jax.experimental import pallas as pl
from jax.experimental.pallas import tpu as pltpu
from jax.sharding import Mesh
from jax.sharding import PartitionSpec as P

DAMPING_RATIO = 0.1
DP = ("x", "zl", "y", "c")
RING = ("x", "zl", "y")
BLOCKS = ("c", "m")
HALF = 256
VMEM = 16 * 1024 * 1024
f32 = jnp.float32
bf16 = jnp.bfloat16


def params():
    return pltpu.CompilerParams(vmem_limit_bytes=VMEM)


def dot(a, b, contract):
    return lax.dot_general(a, b, (contract, ((), ())), preferred_element_type=f32)


def rotate(values, basis):
    return dot(values, basis, ((1,), (0,))).astype(bf16)


def rotate_transposed(values, basis):
    return dot(basis, values, ((0,), (1,))).astype(bf16)


def in_vmem(*arrays):
    return [pltpu.with_memory_space_constraint(a, pltpu.VMEM) for a in arrays]


def local_call(kernel, shapes, scratch=(), scalars=1):
    def call(*operands):
        here = pl.BlockSpec(memory_space=pltpu.VMEM)
        there = pl.BlockSpec(memory_space=pltpu.SMEM)
        return pl.pallas_call(
            kernel,
            in_specs=[there] * scalars + [here] * (len(operands) - scalars),
            out_specs=[here] * len(shapes),
            out_shape=list(shapes),
            scratch_shapes=list(scratch),
            compiler_params=params(),
        )(*operands[:scalars], *in_vmem(*operands[scalars:]))

    return call


def bounds_of(lengths_ref, which):
    result, at = [], jnp.int32(0)
    for j in range(lengths_ref.shape[1]):
        end = at + lengths_ref[which, j]
        result.append((at, end))
        at = end
    return result


def pick(index, values):
    chosen = values[0]
    for j in range(1, len(values)):
        chosen = jnp.where(index == j, values[j], chosen)
    return chosen


def block_curvature(grads, places, masked, wide, finished):
    total = None
    for b in range(2):
        product = dot(grads[b][...], wide[b], ((1,), (0,)))
        total = product * product if total is None else total + product * product
    for b, slot, at in places:
        product = dot(grads[b][:, pl.ds(at, HALF)], masked[slot], ((1,), (0,)))
        total = total + product * product
    finished[...] = total.astype(bf16)
    return jnp.sum(total, axis=0, keepdims=True)


def places_of(lengths_ref):
    count = lengths_ref.shape[1]
    wides, places = [], []
    for b in range(2):
        bounds = bounds_of(lengths_ref, b)
        starts, ends = [v[0] for v in bounds], [v[1] for v in bounds]
        across = jnp.int32(count - 1)
        for j, (start, finish) in enumerate(bounds):
            across = jnp.where((start < HALF) & (finish > HALF), j, across)
        wides.append((pick(across, starts), pick(across, ends)))
        for k in range(count - 1):
            which = k + (k >= across).astype(jnp.int32)
            start = pick(which, starts)
            at = pl.multiple_of(jnp.where(start >= HALF, HALF, 0), HALF)
            places.append((b, b * (count - 1) + k, at, start, pick(which, ends)))
    return wides, places


def near_kernel(lengths_ref, g00, g01, a0_ref, a1_ref, out_hbm, masked, wide, sums_ref, finished, sem):
    acts = (a0_ref, a1_ref)
    tokens, cols = a0_ref.shape
    row = lax.broadcasted_iota(jnp.int32, (HALF, 1), 0)
    rows = lax.broadcasted_iota(jnp.int32, (tokens, 1), 0)
    wides, places = places_of(lengths_ref)
    for b, (start, finish) in enumerate(wides):
        inside = (rows >= start) & (rows < finish)
        wide[b] = jnp.where(inside, acts[b][...], jnp.zeros((tokens, cols), bf16))
    for b, slot, at, start, finish in places:
        inside = (row + at >= start) & (row + at < finish)
        window = acts[b][pl.ds(at, HALF), :]
        masked[slot] = jnp.where(inside, window, jnp.zeros_like(window))
    sums_ref[...] = block_curvature((g00, g01), [p[:3] for p in places], masked, wide, finished)
    width = finished.shape[0]
    copy = pltpu.make_async_copy(finished, out_hbm.at[0:width, 0:cols], sem)
    copy.start()
    copy.wait()


def far_kernel(lengths_ref, _, g10, g11, masked, wide, sums_ref, out_hbm, finished, terms_ref, sems):
    places = places_of(lengths_ref)[1]
    sums = sums_ref[...] + block_curvature((g10, g11), [p[:3] for p in places], masked, wide, finished)
    width, cols = finished.shape
    copy = pltpu.make_async_copy(finished, out_hbm.at[width : 2 * width, 0:cols], sems.at[0])
    copy.start()
    total = jnp.sum(sums, axis=1, keepdims=True)
    high = total.astype(bf16).astype(f32)
    middle = (total - high).astype(bf16).astype(f32)
    low = total - high - middle
    lane = lax.broadcasted_iota(jnp.int32, (1, 128), 1)
    terms = jnp.where(lane == 0, high, jnp.where(lane == 1, middle, jnp.where(lane == 2, low, 0.0)))
    terms_ref[...] = jnp.broadcast_to(terms, terms_ref.shape).astype(bf16)
    also = pltpu.make_async_copy(terms_ref, out_hbm.at[:, cols : cols + 128], sems.at[1])
    also.start()
    copy.wait()
    also.wait()


def near_curvature(lengths, g00, g01, a0, a1):
    width = g00.shape[0]
    tokens, cols = a0.shape
    others = 2 * (lengths.shape[1] - 1)
    here = pl.BlockSpec(memory_space=pltpu.VMEM)
    return pl.pallas_call(
        near_kernel,
        in_specs=[pl.BlockSpec(memory_space=pltpu.SMEM)] + [here] * 4,
        out_specs=[pl.BlockSpec(memory_space=pltpu.HBM), here, here, here],
        out_shape=[
            pltpu.HBM((2 * width, cols + 128), bf16),
            jax.ShapeDtypeStruct((others, HALF, cols), bf16),
            jax.ShapeDtypeStruct((2, tokens, cols), bf16),
            jax.ShapeDtypeStruct((1, cols), f32),
        ],
        scratch_shapes=[pltpu.VMEM((width, cols), bf16), pltpu.SemaphoreType.DMA],
        compiler_params=params(),
    )(lengths, *in_vmem(g00, g01, a0, a1))


def far_curvature(lengths, started, g10, g11, masked, wide, sums):
    width = g10.shape[0]
    cols = sums.shape[1]
    here = pl.BlockSpec(memory_space=pltpu.VMEM)
    anywhere = pl.BlockSpec(memory_space=pltpu.HBM)
    return pl.pallas_call(
        far_kernel,
        in_specs=[pl.BlockSpec(memory_space=pltpu.SMEM), anywhere] + [here] * 5,
        out_specs=anywhere,
        out_shape=pltpu.HBM(started.shape, started.dtype),
        input_output_aliases={1: 0},
        scratch_shapes=[
            pltpu.VMEM((width, cols), bf16),
            pltpu.VMEM((2 * width, 128), bf16),
            pltpu.SemaphoreType.DMA((2,)),
        ],
        compiler_params=params(),
    )(lengths, started, *in_vmem(g10, g11, masked, wide, sums))


def precond_kernel(scale, damping_ref, parts_ref, qg_ref, qa_ref, out_ref):
    cols = qa_ref.shape[1]
    total = parts_ref[0, :, 0:cols].astype(f32)
    for j in range(1, parts_ref.shape[0]):
        total = total + parts_ref[j, :, 0:cols].astype(f32)
    query = dot(qg_ref[...], qa_ref[...], ((1,), (0,)))
    value = (query / (total * scale + damping_ref[0, 0])).astype(bf16)
    for j in range(out_ref.shape[0]):
        out_ref[j] = value


def precond_of(scale, damping, parts, qg, qa):
    shape = (parts.shape[0], parts.shape[1], qa.shape[1])
    return local_call(
        functools.partial(precond_kernel, scale), [jax.ShapeDtypeStruct(shape, bf16)]
    )(damping, parts, qg, qa)[0]


def score_kernel(lengths_ref, p_ref, g00, g01, g10, g11, a0_ref, a1_ref, out_ref):
    width, tokens = g00.shape
    count = lengths_ref.shape[1]
    lane = lax.broadcasted_iota(jnp.int32, (1, tokens), 1)
    line = lax.broadcasted_iota(jnp.int32, (count, 1), 0)
    found = []
    for b, (near, far, acts) in enumerate(((g00, g10, a0_ref), (g01, g11, a1_ref))):
        sums = jnp.zeros((1, tokens), f32)
        for member, grads in enumerate((near, far)):
            product = dot(p_ref[member * width : (member + 1) * width, :], acts[...], ((1,), (1,)))
            sums = sums + jnp.sum(grads[...].astype(f32) * product, axis=0, keepdims=True)
        rows = jnp.zeros((count, 1), f32)
        for j, (start, finish) in enumerate(bounds_of(lengths_ref, b)):
            inside = (lane >= start) & (lane < finish)
            value = jnp.sum(jnp.where(inside, sums, 0.0), axis=1, keepdims=True)
            rows = jnp.where(line == j, value, rows)
        found.append(jnp.broadcast_to(rows, (count, 128)))
    first = lengths_ref[2, 0] == 0
    half = out_ref.shape[0] // 2
    for i in range(half):
        out_ref[i] = jnp.where(first, found[0], found[1])
        out_ref[half + i] = jnp.where(first, found[1], found[0])


def scores_of(lengths, precond, g00, g01, g10, g11, a0, a1):
    shape = (lax.axis_size("c") * lax.axis_size("m"), lengths.shape[1], 128)
    return local_call(score_kernel, [jax.ShapeDtypeStruct(shape, f32)])(
        lengths, precond, g00, g01, g10, g11, a0, a1
    )[0]


def routes(f):
    return [(c * 4 + m, f(c, m)[0] * 4 + f(c, m)[1]) for c in range(2) for m in range(4)]


OTHER_CORE = routes(lambda c, m: (1 - c, m))
GRADS_PARTNER = routes(lambda c, m: (c, m ^ 1))
ACTS_SAME = routes(lambda c, m: (0, m) if c == 0 else (1, 3 - m))
ACTS_OTHER = routes(lambda c, m: (0, m) if c == 1 else (1, 3 - m))


def moved(array, pairs):
    return lax.ppermute(array, BLOCKS, pairs)


def summed(parts, axes):
    return jnp.sum(lax.all_to_all(parts, axes, 0, 0, tiled=True), axis=0)


def shards(train_acts, train_grads, lengths, query_acts, query_grads, basis_in, basis_out):
    ring = lax.axis_index(RING)
    ring_size = lax.axis_size(RING)
    blocks = lax.axis_size("c") * lax.axis_size("m")
    count = lengths.shape[0]

    acts = rotate(train_acts, basis_in)
    acts, train_grads = lax.optimization_barrier((acts, train_grads))
    a1 = moved(acts, ACTS_OTHER)
    a0 = moved(acts, ACTS_SAME)
    g00 = rotate_transposed(train_grads, basis_out)
    other = moved(lengths, OTHER_CORE)
    g00, other, query_acts, query_grads = lax.optimization_barrier((g00, other, query_acts, query_grads))
    g10 = moved(g00, GRADS_PARTNER)
    g01 = moved(g00, OTHER_CORE)
    core = lax.broadcast_in_dim(lax.axis_index("c"), lengths.shape, ())
    both = jnp.stack([lengths, other, core])

    width, cols = g00.shape[0], a0.shape[1]
    chunk = 2 * width // ring_size
    inner = ring_size // 2
    qa = rotate(query_acts, basis_in)
    qg_own = rotate_transposed(query_grads, basis_out)
    qg_mine = lax.dynamic_slice_in_dim(qg_own, lax.rem(ring, inner) * chunk, chunk, 0)
    g10, qa, qg_mine, both = lax.optimization_barrier((g10, qa, qg_mine, both))
    g11 = moved(g10, OTHER_CORE)

    started, masked, wide, sums = near_curvature(both, g00, g01, a0, a1)
    sums, qa, qg_mine = lax.optimization_barrier((sums, qa, qg_mine))
    qa = moved(qa, ACTS_OTHER)
    qg_far = moved(qg_mine, GRADS_PARTNER)
    curvature = far_curvature(both, started, g10, g11, masked, wide, sums)
    curvature, qa, qg_far = lax.optimization_barrier((curvature, qa, qg_far))
    qg = jnp.where(ring < inner, qg_mine, qg_far)
    parts = lax.all_to_all(curvature.reshape(ring_size, chunk, cols + 128), RING, 0, 0, tiled=True)
    total = jnp.sum(parts[:, 0, cols : cols + 3].astype(f32))
    total = summed(jnp.broadcast_to(total, (blocks, 1, 1)), BLOCKS)
    scale = 1.0 / (count * lax.axis_size(DP))
    entries = 2 * width * cols * blocks
    damping = total * (DAMPING_RATIO * scale / entries)

    mine = precond_of(scale, damping, parts, qg, qa)
    precond = lax.all_to_all(mine, RING, 0, 0, tiled=True).reshape(2 * width, cols)
    found = scores_of(both, precond, g00, g01, g10, g11, a0, a1)
    return summed(found, BLOCKS)[:, 0].reshape(1, count)


def solution(mesh):
    cut = Mesh(np.asarray(mesh.devices).reshape(4, 2, 4, 2, 4), ("x", "zl", "y", "c", "m"))
    return jax.shard_map(
        shards,
        mesh=cut,
        in_specs=(P(DP, None), P(DP, None), P(DP), P(), P(), P(None, "m"), P(None, "m")),
        out_specs=P(None, DP),
        check_vma=False,
    )
```

```python
import functools

import jax
import jax.numpy as jnp
import numpy as np
from jax import lax
from jax.experimental import pallas as pl
from jax.experimental.pallas import tpu as pltpu
from jax.sharding import Mesh
from jax.sharding import PartitionSpec as P

DAMPING_RATIO = 0.1
DP = ("x", "zl", "y", "c")
RING = ("x", "zl", "y")
BLOCKS = ("c", "m")
HALF = 256
VMEM = 16 * 1024 * 1024
f32 = jnp.float32
bf16 = jnp.bfloat16


def params():
    return pltpu.CompilerParams(vmem_limit_bytes=VMEM)


def dot(a, b, contract):
    return lax.dot_general(a, b, (contract, ((), ())), preferred_element_type=f32)


def rotate(values, basis):
    return dot(values, basis, ((1,), (0,))).astype(bf16)


def rotate_transposed(values, basis):
    return dot(basis, values, ((0,), (1,))).astype(bf16)


def in_vmem(*arrays):
    return [pltpu.with_memory_space_constraint(a, pltpu.VMEM) for a in arrays]


def local_call(kernel, shapes, scratch=(), scalars=1):
    def call(*operands):
        here = pl.BlockSpec(memory_space=pltpu.VMEM)
        there = pl.BlockSpec(memory_space=pltpu.SMEM)
        return pl.pallas_call(
            kernel,
            in_specs=[there] * scalars + [here] * (len(operands) - scalars),
            out_specs=[here] * len(shapes),
            out_shape=list(shapes),
            scratch_shapes=list(scratch),
            compiler_params=params(),
        )(*operands[:scalars], *in_vmem(*operands[scalars:]))

    return call


def bounds_of(lengths_ref, which):
    result, at = [], jnp.int32(0)
    for j in range(lengths_ref.shape[1]):
        end = at + lengths_ref[which, j]
        result.append((at, end))
        at = end
    return result


def pick(index, values):
    chosen = values[0]
    for j in range(1, len(values)):
        chosen = jnp.where(index == j, values[j], chosen)
    return chosen


def block_curvature(grads, places, masked, wide, finished):
    total = None
    for b in range(2):
        product = dot(grads[b][...], wide[b], ((1,), (0,)))
        total = product * product if total is None else total + product * product
    for b, slot, at in places:
        product = dot(grads[b][:, pl.ds(at, HALF)], masked[slot], ((1,), (0,)))
        total = total + product * product
    finished[...] = total.astype(bf16)
    return jnp.sum(total, axis=0, keepdims=True)


def places_of(lengths_ref):
    count = lengths_ref.shape[1]
    wides, places = [], []
    for b in range(2):
        bounds = bounds_of(lengths_ref, b)
        starts, ends = [v[0] for v in bounds], [v[1] for v in bounds]
        across = jnp.int32(count - 1)
        for j, (start, finish) in enumerate(bounds):
            across = jnp.where((start < HALF) & (finish > HALF), j, across)
        wides.append((pick(across, starts), pick(across, ends)))
        for k in range(count - 1):
            which = k + (k >= across).astype(jnp.int32)
            start = pick(which, starts)
            at = pl.multiple_of(jnp.where(start >= HALF, HALF, 0), HALF)
            places.append((b, b * (count - 1) + k, at, start, pick(which, ends)))
    return wides, places


def curvature_kernel(
    lengths_ref, g00, g01, g10, g11, a0_ref, a1_ref, out_hbm, masked, wide, near, far, terms_ref, sems
):
    acts = (a0_ref, a1_ref)
    tokens, cols = a0_ref.shape
    width = g00.shape[0]
    row = lax.broadcasted_iota(jnp.int32, (HALF, 1), 0)
    rows = lax.broadcasted_iota(jnp.int32, (tokens, 1), 0)
    wides, places = places_of(lengths_ref)
    for b, (start, finish) in enumerate(wides):
        inside = (rows >= start) & (rows < finish)
        wide[b] = jnp.where(inside, acts[b][...], jnp.zeros((tokens, cols), bf16))
    for b, slot, at, start, finish in places:
        inside = (row + at >= start) & (row + at < finish)
        window = acts[b][pl.ds(at, HALF), :]
        masked[slot] = jnp.where(inside, window, jnp.zeros_like(window))
    places = [p[:3] for p in places]
    sums = block_curvature((g00, g01), places, masked, wide, near)
    first = pltpu.make_async_copy(near, out_hbm.at[0:width, 0:cols], sems.at[0])
    first.start()
    sums = sums + block_curvature((g10, g11), places, masked, wide, far)
    second = pltpu.make_async_copy(far, out_hbm.at[width : 2 * width, 0:cols], sems.at[1])
    second.start()
    total = jnp.sum(sums, axis=1, keepdims=True)
    high = total.astype(bf16).astype(f32)
    middle = (total - high).astype(bf16).astype(f32)
    low = total - high - middle
    lane = lax.broadcasted_iota(jnp.int32, (1, 128), 1)
    terms = jnp.where(lane == 0, high, jnp.where(lane == 1, middle, jnp.where(lane == 2, low, 0.0)))
    terms_ref[...] = jnp.broadcast_to(terms, terms_ref.shape).astype(bf16)
    third = pltpu.make_async_copy(terms_ref, out_hbm.at[:, cols : cols + 128], sems.at[2])
    third.start()
    first.wait()
    second.wait()
    third.wait()


def curvature_of(lengths, g00, g01, g10, g11, a0, a1):
    width = g00.shape[0]
    tokens, cols = a0.shape
    others = 2 * (lengths.shape[1] - 1)
    here = pl.BlockSpec(memory_space=pltpu.VMEM)
    return pl.pallas_call(
        curvature_kernel,
        in_specs=[pl.BlockSpec(memory_space=pltpu.SMEM)] + [here] * 6,
        out_specs=pl.BlockSpec(memory_space=pltpu.HBM),
        out_shape=pltpu.HBM((2 * width, cols + 128), bf16),
        scratch_shapes=[
            pltpu.VMEM((others, HALF, cols), bf16),
            pltpu.VMEM((2, tokens, cols), bf16),
            pltpu.VMEM((width, cols), bf16),
            pltpu.VMEM((width, cols), bf16),
            pltpu.VMEM((2 * width, 128), bf16),
            pltpu.SemaphoreType.DMA((3,)),
        ],
        compiler_params=params(),
    )(lengths, *in_vmem(g00, g01, g10, g11, a0, a1))


def precond_kernel(scale, damping_ref, parts_ref, qg_ref, qa_ref, out_ref):
    cols = qa_ref.shape[1]
    total = parts_ref[0, :, 0:cols].astype(f32)
    for j in range(1, parts_ref.shape[0]):
        total = total + parts_ref[j, :, 0:cols].astype(f32)
    query = dot(qg_ref[...], qa_ref[...], ((1,), (0,)))
    value = (query / (total * scale + damping_ref[0, 0])).astype(bf16)
    for j in range(out_ref.shape[0]):
        out_ref[j] = value


def precond_of(scale, damping, parts, qg, qa):
    shape = (parts.shape[0], parts.shape[1], qa.shape[1])
    return local_call(
        functools.partial(precond_kernel, scale), [jax.ShapeDtypeStruct(shape, bf16)]
    )(damping, parts, qg, qa)[0]


def score_kernel(lengths_ref, p_ref, g00, g01, g10, g11, a0_ref, a1_ref, out_ref):
    width, tokens = g00.shape
    count = lengths_ref.shape[1]
    lane = lax.broadcasted_iota(jnp.int32, (1, tokens), 1)
    line = lax.broadcasted_iota(jnp.int32, (count, 1), 0)
    found = []
    for b, (near, far, acts) in enumerate(((g00, g10, a0_ref), (g01, g11, a1_ref))):
        sums = jnp.zeros((1, tokens), f32)
        for member, grads in enumerate((near, far)):
            product = dot(p_ref[member * width : (member + 1) * width, :], acts[...], ((1,), (1,)))
            sums = sums + jnp.sum(grads[...].astype(f32) * product, axis=0, keepdims=True)
        rows = jnp.zeros((count, 1), f32)
        for j, (start, finish) in enumerate(bounds_of(lengths_ref, b)):
            inside = (lane >= start) & (lane < finish)
            value = jnp.sum(jnp.where(inside, sums, 0.0), axis=1, keepdims=True)
            rows = jnp.where(line == j, value, rows)
        found.append(jnp.broadcast_to(rows, (count, 128)))
    first = lengths_ref[2, 0] == 0
    half = out_ref.shape[0] // 2
    for i in range(half):
        out_ref[i] = jnp.where(first, found[0], found[1])
        out_ref[half + i] = jnp.where(first, found[1], found[0])


def scores_of(lengths, precond, g00, g01, g10, g11, a0, a1):
    shape = (lax.axis_size("c") * lax.axis_size("m"), lengths.shape[1], 128)
    return local_call(score_kernel, [jax.ShapeDtypeStruct(shape, f32)])(
        lengths, precond, g00, g01, g10, g11, a0, a1
    )[0]


def routes(f):
    return [(c * 4 + m, f(c, m)[0] * 4 + f(c, m)[1]) for c in range(2) for m in range(4)]


OTHER_CORE = routes(lambda c, m: (1 - c, m))
GRADS_PARTNER = routes(lambda c, m: (c, m ^ 1))
ACTS_SAME = routes(lambda c, m: (0, m) if c == 0 else (1, 3 - m))
ACTS_OTHER = routes(lambda c, m: (0, m) if c == 1 else (1, 3 - m))


def moved(array, pairs):
    return lax.ppermute(array, BLOCKS, pairs)


def summed(parts, axes):
    return jnp.sum(lax.all_to_all(parts, axes, 0, 0, tiled=True), axis=0)


def shards(train_acts, train_grads, lengths, query_acts, query_grads, basis_in, basis_out):
    ring = lax.axis_index(RING)
    ring_size = lax.axis_size(RING)
    blocks = lax.axis_size("c") * lax.axis_size("m")
    count = lengths.shape[0]

    other = moved(lengths, OTHER_CORE)
    g00 = rotate_transposed(train_grads, basis_out)
    g00, other, train_acts = lax.optimization_barrier((g00, other, train_acts))
    g10 = moved(g00, GRADS_PARTNER)
    g01 = moved(g00, OTHER_CORE)
    acts = rotate(train_acts, basis_in)
    acts, g01, query_acts, query_grads = lax.optimization_barrier((acts, g01, query_acts, query_grads))
    a1 = moved(acts, ACTS_OTHER)
    a0 = moved(acts, ACTS_SAME)
    core = lax.broadcast_in_dim(lax.axis_index("c"), lengths.shape, ())
    both = jnp.stack([lengths, other, core])

    width, cols = g00.shape[0], a0.shape[1]
    chunk = 2 * width // ring_size
    inner = ring_size // 2
    qa = rotate(query_acts, basis_in)
    qg_own = rotate_transposed(query_grads, basis_out)
    qg_mine = lax.dynamic_slice_in_dim(qg_own, lax.rem(ring, inner) * chunk, chunk, 0)
    g10, qa, qg_mine, both = lax.optimization_barrier((g10, qa, qg_mine, both))
    g11 = moved(g10, OTHER_CORE)
    a0, a1, qa, qg_mine = lax.optimization_barrier((a0, a1, qa, qg_mine))
    qa = moved(qa, ACTS_OTHER)
    qg_far = moved(qg_mine, GRADS_PARTNER)
    curvature = curvature_of(both, g00, g01, g10, g11, a0, a1)
    curvature, qa, qg_far = lax.optimization_barrier((curvature, qa, qg_far))
    qg = jnp.where(ring < inner, qg_mine, qg_far)
    parts = lax.all_to_all(curvature.reshape(ring_size, chunk, cols + 128), RING, 0, 0, tiled=True)
    total = jnp.sum(parts[:, 0, cols : cols + 3].astype(f32))
    total = summed(jnp.broadcast_to(total, (blocks, 1, 1)), BLOCKS)
    scale = 1.0 / (count * lax.axis_size(DP))
    entries = 2 * width * cols * blocks
    damping = total * (DAMPING_RATIO * scale / entries)

    mine = precond_of(scale, damping, parts, qg, qa)
    precond = lax.all_to_all(mine, RING, 0, 0, tiled=True).reshape(2 * width, cols)
    found = scores_of(both, precond, g00, g01, g10, g11, a0, a1)
    return summed(found, BLOCKS)[:, 0].reshape(1, count)


def solution(mesh):
    cut = Mesh(np.asarray(mesh.devices).reshape(4, 2, 4, 2, 4), ("x", "zl", "y", "c", "m"))
    return jax.shard_map(
        shards,
        mesh=cut,
        in_specs=(P(DP, None), P(DP, None), P(DP), P(), P(), P(None, "m"), P(None, "m")),
        out_specs=P(None, DP),
        check_vma=False,
    )
```

```python
import functools

import jax
import jax.numpy as jnp
import numpy as np
from jax import lax
from jax.experimental import pallas as pl
from jax.experimental.pallas import tpu as pltpu
from jax.sharding import Mesh
from jax.sharding import PartitionSpec as P

DAMPING_RATIO = 0.1
DP = ("x", "zl", "y", "c")
RING = ("x", "zl", "y")
BLOCKS = ("c", "m")
HALF = 256
VMEM = 16 * 1024 * 1024
f32 = jnp.float32
bf16 = jnp.bfloat16


def params():
    return pltpu.CompilerParams(vmem_limit_bytes=VMEM)


def dot(a, b, contract):
    return lax.dot_general(a, b, (contract, ((), ())), preferred_element_type=f32)


def rotate(values, basis):
    return dot(values, basis, ((1,), (0,))).astype(bf16)


def rotate_transposed(values, basis):
    return dot(basis, values, ((0,), (1,))).astype(bf16)


def in_vmem(*arrays):
    return [pltpu.with_memory_space_constraint(a, pltpu.VMEM) for a in arrays]


def local_call(kernel, shapes, scratch=(), scalars=1):
    def call(*operands):
        here = pl.BlockSpec(memory_space=pltpu.VMEM)
        there = pl.BlockSpec(memory_space=pltpu.SMEM)
        return pl.pallas_call(
            kernel,
            in_specs=[there] * scalars + [here] * (len(operands) - scalars),
            out_specs=[here] * len(shapes),
            out_shape=list(shapes),
            scratch_shapes=list(scratch),
            compiler_params=params(),
        )(*operands[:scalars], *in_vmem(*operands[scalars:]))

    return call


def bounds_of(lengths_ref, which):
    result, at = [], jnp.int32(0)
    for j in range(lengths_ref.shape[1]):
        end = at + lengths_ref[which, j]
        result.append((at, end))
        at = end
    return result


def pick(index, values):
    chosen = values[0]
    for j in range(1, len(values)):
        chosen = jnp.where(index == j, values[j], chosen)
    return chosen


def block_curvature(grads, places, masked, wide, finished):
    total = None
    for b in range(2):
        product = dot(grads[b][...], wide[b], ((1,), (0,)))
        total = product * product if total is None else total + product * product
    for b, slot, at in places:
        product = dot(grads[b][:, pl.ds(at, HALF)], masked[slot], ((1,), (0,)))
        total = total + product * product
    finished[...] = total.astype(bf16)
    return jnp.sum(total, axis=0, keepdims=True)


def places_of(lengths_ref):
    count = lengths_ref.shape[1]
    wides, places = [], []
    for b in range(2):
        bounds = bounds_of(lengths_ref, b)
        starts, ends = [v[0] for v in bounds], [v[1] for v in bounds]
        across = jnp.int32(count - 1)
        for j, (start, finish) in enumerate(bounds):
            across = jnp.where((start < HALF) & (finish > HALF), j, across)
        wides.append((pick(across, starts), pick(across, ends)))
        for k in range(count - 1):
            which = k + (k >= across).astype(jnp.int32)
            start = pick(which, starts)
            at = pl.multiple_of(jnp.where(start >= HALF, HALF, 0), HALF)
            places.append((b, b * (count - 1) + k, at, start, pick(which, ends)))
    return wides, places


def curvature_kernel(
    lengths_ref, g00, g01, g10, g11, a0_ref, a1_ref, out_hbm, masked, wide, near, far, terms_ref, sems
):
    acts = (a0_ref, a1_ref)
    tokens, cols = a0_ref.shape
    width = g00.shape[0]
    row = lax.broadcasted_iota(jnp.int32, (HALF, 1), 0)
    rows = lax.broadcasted_iota(jnp.int32, (tokens, 1), 0)
    wides, places = places_of(lengths_ref)
    for b, (start, finish) in enumerate(wides):
        inside = (rows >= start) & (rows < finish)
        wide[b] = jnp.where(inside, acts[b][...], jnp.zeros((tokens, cols), bf16))
    for b, slot, at, start, finish in places:
        inside = (row + at >= start) & (row + at < finish)
        window = acts[b][pl.ds(at, HALF), :]
        masked[slot] = jnp.where(inside, window, jnp.zeros_like(window))
    places = [p[:3] for p in places]
    sums = block_curvature((g00, g01), places, masked, wide, near)
    first = pltpu.make_async_copy(near, out_hbm.at[0:width, 0:cols], sems.at[0])
    first.start()
    sums = sums + block_curvature((g10, g11), places, masked, wide, far)
    second = pltpu.make_async_copy(far, out_hbm.at[width : 2 * width, 0:cols], sems.at[1])
    second.start()
    total = jnp.sum(sums, axis=1, keepdims=True)
    high = total.astype(bf16).astype(f32)
    middle = (total - high).astype(bf16).astype(f32)
    low = total - high - middle
    lane = lax.broadcasted_iota(jnp.int32, (1, 128), 1)
    terms = jnp.where(lane == 0, high, jnp.where(lane == 1, middle, jnp.where(lane == 2, low, 0.0)))
    terms_ref[...] = jnp.broadcast_to(terms, terms_ref.shape).astype(bf16)
    third = pltpu.make_async_copy(terms_ref, out_hbm.at[:, cols : cols + 128], sems.at[2])
    third.start()
    first.wait()
    second.wait()
    third.wait()


def curvature_of(lengths, g00, g01, g10, g11, a0, a1):
    width = g00.shape[0]
    tokens, cols = a0.shape
    others = 2 * (lengths.shape[1] - 1)
    here = pl.BlockSpec(memory_space=pltpu.VMEM)
    return pl.pallas_call(
        curvature_kernel,
        in_specs=[pl.BlockSpec(memory_space=pltpu.SMEM)] + [here] * 6,
        out_specs=pl.BlockSpec(memory_space=pltpu.HBM),
        out_shape=pltpu.HBM((2 * width, cols + 128), bf16),
        scratch_shapes=[
            pltpu.VMEM((others, HALF, cols), bf16),
            pltpu.VMEM((2, tokens, cols), bf16),
            pltpu.VMEM((width, cols), bf16),
            pltpu.VMEM((width, cols), bf16),
            pltpu.VMEM((2 * width, 128), bf16),
            pltpu.SemaphoreType.DMA((3,)),
        ],
        compiler_params=params(),
    )(lengths, *in_vmem(g00, g01, g10, g11, a0, a1))


def reduce_kernel(parts_ref, chunk_ref, total_ref):
    cols = chunk_ref.shape[1]
    chunk = parts_ref[0, :, 0:cols].astype(f32)
    terms = parts_ref[0, 0:8, cols:].astype(f32)
    for j in range(1, parts_ref.shape[0]):
        chunk = chunk + parts_ref[j, :, 0:cols].astype(f32)
        terms = terms + parts_ref[j, 0:8, cols:].astype(f32)
    chunk_ref[...] = chunk
    total_ref[...] = jnp.broadcast_to(jnp.sum(terms, axis=1, keepdims=True), total_ref.shape)


def reduced(parts, cols):
    shapes = [(parts.shape[1], cols), (8, 128)]
    return local_call(
        reduce_kernel, [jax.ShapeDtypeStruct(s, f32) for s in shapes], scalars=0
    )(parts)


def precond_kernel(scale, damping_scale, chunk_ref, total_ref, more_ref, qg_ref, qa_ref, out_ref):
    damping = (total_ref[0:1, 0:1] + more_ref[0:1, 0:1]) * damping_scale
    query = dot(qg_ref[...], qa_ref[...], ((1,), (0,)))
    value = (query / (chunk_ref[...] * scale + damping)).astype(bf16)
    for j in range(out_ref.shape[0]):
        out_ref[j] = value


def precond_of(copies, scale, damping_scale, chunk, total, more, qg, qa):
    shape = (copies, *chunk.shape)
    return local_call(
        functools.partial(precond_kernel, scale, damping_scale), [jax.ShapeDtypeStruct(shape, bf16)], scalars=0
    )(chunk, total, more, qg, qa)[0]


def score_kernel(lengths_ref, p_ref, g00, g01, g10, g11, a0_ref, a1_ref, out_ref):
    width, tokens = g00.shape
    count = lengths_ref.shape[1]
    lane = lax.broadcasted_iota(jnp.int32, (1, tokens), 1)
    line = lax.broadcasted_iota(jnp.int32, (count, 1), 0)
    found = []
    for b, (near, far, acts) in enumerate(((g00, g10, a0_ref), (g01, g11, a1_ref))):
        sums = jnp.zeros((1, tokens), f32)
        for member, grads in enumerate((near, far)):
            product = dot(p_ref[member * width : (member + 1) * width, :], acts[...], ((1,), (1,)))
            sums = sums + jnp.sum(grads[...].astype(f32) * product, axis=0, keepdims=True)
        rows = jnp.zeros((count, 1), f32)
        for j, (start, finish) in enumerate(bounds_of(lengths_ref, b)):
            inside = (lane >= start) & (lane < finish)
            value = jnp.sum(jnp.where(inside, sums, 0.0), axis=1, keepdims=True)
            rows = jnp.where(line == j, value, rows)
        found.append(jnp.broadcast_to(rows, (count, 128)))
    first = lengths_ref[2, 0] == 0
    half = out_ref.shape[0] // 2
    for i in range(half):
        out_ref[i] = jnp.where(first, found[0], found[1])
        out_ref[half + i] = jnp.where(first, found[1], found[0])


def scores_of(lengths, precond, g00, g01, g10, g11, a0, a1):
    shape = (lax.axis_size("c") * lax.axis_size("m"), lengths.shape[1], 128)
    return local_call(score_kernel, [jax.ShapeDtypeStruct(shape, f32)])(
        lengths, precond, g00, g01, g10, g11, a0, a1
    )[0]


def routes(f):
    return [(c * 4 + m, f(c, m)[0] * 4 + f(c, m)[1]) for c in range(2) for m in range(4)]


OTHER_CORE = routes(lambda c, m: (1 - c, m))
GRADS_PARTNER = routes(lambda c, m: (c, m ^ 1))
ACTS_PARTNER = routes(lambda c, m: (c, 3 - m))
ACTS_SAME = routes(lambda c, m: (0, m) if c == 0 else (1, 3 - m))
ACTS_OTHER = routes(lambda c, m: (0, m) if c == 1 else (1, 3 - m))


def moved(array, pairs):
    return lax.ppermute(array, BLOCKS, pairs)


def summed(parts, axes):
    return jnp.sum(lax.all_to_all(parts, axes, 0, 0, tiled=True), axis=0)


def shards(train_acts, train_grads, lengths, query_acts, query_grads, basis_in, basis_out):
    ring = lax.axis_index(RING)
    ring_size = lax.axis_size(RING)
    blocks = lax.axis_size("c") * lax.axis_size("m")
    count = lengths.shape[0]

    other = moved(lengths, OTHER_CORE)
    g00 = rotate_transposed(train_grads, basis_out)
    g00, other, train_acts = lax.optimization_barrier((g00, other, train_acts))
    g10 = moved(g00, GRADS_PARTNER)
    g01 = moved(g00, OTHER_CORE)
    acts = rotate(train_acts, basis_in)
    acts, g01, query_acts, query_grads = lax.optimization_barrier((acts, g01, query_acts, query_grads))
    a1 = moved(acts, ACTS_OTHER)
    a0 = moved(acts, ACTS_SAME)
    core = lax.broadcast_in_dim(lax.axis_index("c"), lengths.shape, ())
    both = jnp.stack([lengths, other, core])

    width, cols = g00.shape[0], a0.shape[1]
    chunk = 2 * width // ring_size
    inner = ring_size // 2
    qa = rotate(query_acts, basis_in)
    qg_own = rotate_transposed(query_grads, basis_out)
    qg_mine = lax.dynamic_slice_in_dim(qg_own, lax.rem(ring, inner) * chunk, chunk, 0)
    g10, qa, qg_mine, both = lax.optimization_barrier((g10, qa, qg_mine, both))
    g11 = moved(g10, OTHER_CORE)
    qa = moved(qa, ACTS_OTHER)
    qg_far = moved(qg_mine, GRADS_PARTNER)
    curvature = curvature_of(both, g00, g01, g10, g11, a0, a1)
    curvature, qa, qg_far = lax.optimization_barrier((curvature, qa, qg_far))
    qg = jnp.where(ring < inner, qg_mine, qg_far)
    parts = lax.all_to_all(curvature.reshape(ring_size, chunk, cols + 128), RING, 0, 0, tiled=True)
    mine, total = reduced(parts, cols)
    total = total + moved(total, OTHER_CORE)
    total = total + moved(total, GRADS_PARTNER)
    more = moved(total, ACTS_PARTNER)
    scale = 1.0 / (count * lax.axis_size(DP))
    damping_scale = DAMPING_RATIO * scale / (2 * width * cols * blocks)
    mine = precond_of(ring_size, scale, damping_scale, mine, total, more, qg, qa)
    precond = lax.all_to_all(mine, RING, 0, 0, tiled=True).reshape(2 * width, cols)
    found = scores_of(both, precond, g00, g01, g10, g11, a0, a1)
    return summed(found, BLOCKS)[:, 0].reshape(1, count)


def solution(mesh):
    cut = Mesh(np.asarray(mesh.devices).reshape(4, 2, 4, 2, 4), ("x", "zl", "y", "c", "m"))
    return jax.shard_map(
        shards,
        mesh=cut,
        in_specs=(P(DP, None), P(DP, None), P(DP), P(), P(), P(None, "m"), P(None, "m")),
        out_specs=P(None, DP),
        check_vma=False,
    )
```

```python
import functools

import jax
import jax.numpy as jnp
import numpy as np
from jax import lax
from jax.experimental import pallas as pl
from jax.experimental.pallas import tpu as pltpu
from jax.sharding import Mesh
from jax.sharding import PartitionSpec as P

DAMPING_RATIO = 0.1
DP = ("x", "zl", "y", "c")
RING = ("x", "zl", "y")
BLOCKS = ("c", "m")
HALF = 256
LANES = 128
SPARE = 8
VMEM = 16 * 1024 * 1024
f32 = jnp.float32
bf16 = jnp.bfloat16


def params():
    return pltpu.CompilerParams(vmem_limit_bytes=VMEM)


def dot(a, b, contract):
    return lax.dot_general(a, b, (contract, ((), ())), preferred_element_type=f32)


def rotate(values, basis):
    return dot(values, basis, ((1,), (0,))).astype(bf16)


def rotate_transposed(values, basis):
    return dot(basis, values, ((0,), (1,))).astype(bf16)


def in_vmem(*arrays):
    return [pltpu.with_memory_space_constraint(a, pltpu.VMEM) for a in arrays]


def local_call(kernel, shapes, scratch=(), scalars=1):
    def call(*operands):
        here = pl.BlockSpec(memory_space=pltpu.VMEM)
        there = pl.BlockSpec(memory_space=pltpu.SMEM)
        return pl.pallas_call(
            kernel,
            in_specs=[there] * scalars + [here] * (len(operands) - scalars),
            out_specs=[here] * len(shapes),
            out_shape=list(shapes),
            scratch_shapes=list(scratch),
            compiler_params=params(),
        )(*operands[:scalars], *in_vmem(*operands[scalars:]))

    return call


def bounds_of(lengths_ref, which):
    result, at = [], jnp.int32(0)
    for j in range(lengths_ref.shape[1]):
        end = at + lengths_ref[which, j]
        result.append((at, end))
        at = end
    return result


def pick(index, values):
    chosen = values[0]
    for j in range(1, len(values)):
        chosen = jnp.where(index == j, values[j], chosen)
    return chosen


def block_curvature(grads, places, masked, wide, out_ref, first):
    total = None
    for b in range(2):
        product = dot(grads[b][...], wide[b], ((1,), (0,)))
        total = product * product if total is None else total + product * product
    for b, slot, at in places:
        product = dot(grads[b][:, pl.ds(at, HALF)], masked[slot], ((1,), (0,)))
        total = total + product * product
    rows, cols = total.shape
    chunk = (out_ref.shape[1] - SPARE) * LANES // cols
    spare = jnp.zeros((SPARE, LANES), f32)
    for k in range(rows // chunk):
        block = total[k * chunk : (k + 1) * chunk]
        pieces = [block[:, j * LANES : (j + 1) * LANES] for j in range(cols // LANES)]
        out_ref[first + k] = jnp.concatenate([*pieces, spare], axis=0).astype(bf16)
    return jnp.sum(total, axis=0, keepdims=True)


def places_of(lengths_ref):
    count = lengths_ref.shape[1]
    wides, places = [], []
    for b in range(2):
        bounds = bounds_of(lengths_ref, b)
        starts, ends = [v[0] for v in bounds], [v[1] for v in bounds]
        across = jnp.int32(count - 1)
        for j, (start, finish) in enumerate(bounds):
            across = jnp.where((start < HALF) & (finish > HALF), j, across)
        wides.append((pick(across, starts), pick(across, ends)))
        for k in range(count - 1):
            which = k + (k >= across).astype(jnp.int32)
            start = pick(which, starts)
            at = pl.multiple_of(jnp.where(start >= HALF, HALF, 0), HALF)
            places.append((b, b * (count - 1) + k, at, start, pick(which, ends)))
    return wides, places


def curvature_kernel(lengths_ref, g00, g01, g10, g11, a0_ref, a1_ref, out_ref, masked, wide):
    acts = (a0_ref, a1_ref)
    tokens, cols = a0_ref.shape
    row = lax.broadcasted_iota(jnp.int32, (HALF, 1), 0)
    rows = lax.broadcasted_iota(jnp.int32, (tokens, 1), 0)
    wides, places = places_of(lengths_ref)
    for b, (start, finish) in enumerate(wides):
        inside = (rows >= start) & (rows < finish)
        wide[b] = jnp.where(inside, acts[b][...], jnp.zeros((tokens, cols), bf16))
    for b, slot, at, start, finish in places:
        inside = (row + at >= start) & (row + at < finish)
        window = acts[b][pl.ds(at, HALF), :]
        masked[slot] = jnp.where(inside, window, jnp.zeros_like(window))
    places = [p[:3] for p in places]
    sums = block_curvature((g00, g01), places, masked, wide, out_ref, 0)
    sums = sums + block_curvature((g10, g11), places, masked, wide, out_ref, out_ref.shape[0] // 2)
    total = jnp.sum(sums, axis=1, keepdims=True)
    high = total.astype(bf16).astype(f32)
    middle = (total - high).astype(bf16).astype(f32)
    low = total - high - middle
    lane = lax.broadcasted_iota(jnp.int32, (1, LANES), 1)
    terms = jnp.where(lane == 0, high, jnp.where(lane == 1, middle, jnp.where(lane == 2, low, 0.0)))
    terms = jnp.broadcast_to(terms, (SPARE, LANES))
    last = out_ref.shape[1] - 2 * SPARE
    for k in range(out_ref.shape[0]):
        end = out_ref[k, last:, :].astype(f32)
        out_ref[k, last:, :] = jnp.concatenate([end[0:SPARE], terms], axis=0).astype(bf16)


def curvature_of(chunks, lengths, g00, g01, g10, g11, a0, a1):
    width = g00.shape[0]
    tokens, cols = a0.shape
    others = 2 * (lengths.shape[1] - 1)
    shape = (chunks, 2 * width * cols // (chunks * LANES) + SPARE, LANES)
    return local_call(
        curvature_kernel,
        [jax.ShapeDtypeStruct(shape, bf16)],
        [pltpu.VMEM((others, HALF, cols), bf16), pltpu.VMEM((2, tokens, cols), bf16)],
    )(lengths, g00, g01, g10, g11, a0, a1)[0]


def reduce_kernel(parts_ref, chunk_ref, total_ref):
    rows, cols = chunk_ref.shape
    found = parts_ref[0].astype(f32)
    for j in range(1, parts_ref.shape[0]):
        found = found + parts_ref[j].astype(f32)
    pieces = [found[j * rows : (j + 1) * rows] for j in range(cols // LANES)]
    chunk_ref[...] = jnp.concatenate(pieces, axis=1)
    terms = found[found.shape[0] - SPARE :]
    total_ref[...] = jnp.broadcast_to(jnp.sum(terms, axis=1, keepdims=True), total_ref.shape)


def reduced(parts, cols):
    shapes = [((parts.shape[1] - SPARE) * LANES // cols, cols), (SPARE, LANES)]
    return local_call(
        reduce_kernel, [jax.ShapeDtypeStruct(s, f32) for s in shapes], scalars=0
    )(parts)


def precond_kernel(scale, damping_scale, chunk_ref, total_ref, more_ref, qg_ref, qa_ref, out_ref):
    damping = (total_ref[0:1, 0:1] + more_ref[0:1, 0:1]) * damping_scale
    query = dot(qg_ref[...], qa_ref[...], ((1,), (0,)))
    value = (query / (chunk_ref[...] * scale + damping)).astype(bf16)
    for j in range(out_ref.shape[0]):
        out_ref[j] = value


def precond_of(copies, scale, damping_scale, chunk, total, more, qg, qa):
    shape = (copies, *chunk.shape)
    return local_call(
        functools.partial(precond_kernel, scale, damping_scale), [jax.ShapeDtypeStruct(shape, bf16)], scalars=0
    )(chunk, total, more, qg, qa)[0]


def score_kernel(lengths_ref, p_ref, g00, g01, g10, g11, a0_ref, a1_ref, out_ref):
    width, tokens = g00.shape
    count = lengths_ref.shape[1]
    lane = lax.broadcasted_iota(jnp.int32, (1, tokens), 1)
    line = lax.broadcasted_iota(jnp.int32, (count, 1), 0)
    found = []
    for b, (near, far, acts) in enumerate(((g00, g10, a0_ref), (g01, g11, a1_ref))):
        sums = jnp.zeros((1, tokens), f32)
        for member, grads in enumerate((near, far)):
            product = dot(p_ref[member * width : (member + 1) * width, :], acts[...], ((1,), (1,)))
            sums = sums + jnp.sum(grads[...].astype(f32) * product, axis=0, keepdims=True)
        rows = jnp.zeros((count, 1), f32)
        for j, (start, finish) in enumerate(bounds_of(lengths_ref, b)):
            inside = (lane >= start) & (lane < finish)
            value = jnp.sum(jnp.where(inside, sums, 0.0), axis=1, keepdims=True)
            rows = jnp.where(line == j, value, rows)
        found.append(jnp.broadcast_to(rows, (count, 128)))
    first = lengths_ref[2, 0] == 0
    half = out_ref.shape[0] // 2
    for i in range(half):
        out_ref[i] = jnp.where(first, found[0], found[1])
        out_ref[half + i] = jnp.where(first, found[1], found[0])


def scores_of(lengths, precond, g00, g01, g10, g11, a0, a1):
    shape = (lax.axis_size("c") * lax.axis_size("m"), lengths.shape[1], 128)
    return local_call(score_kernel, [jax.ShapeDtypeStruct(shape, f32)])(
        lengths, precond, g00, g01, g10, g11, a0, a1
    )[0]


def routes(f):
    return [(c * 4 + m, f(c, m)[0] * 4 + f(c, m)[1]) for c in range(2) for m in range(4)]


OTHER_CORE = routes(lambda c, m: (1 - c, m))
GRADS_PARTNER = routes(lambda c, m: (c, m ^ 1))
ACTS_PARTNER = routes(lambda c, m: (c, 3 - m))
ACTS_SAME = routes(lambda c, m: (0, m) if c == 0 else (1, 3 - m))
ACTS_OTHER = routes(lambda c, m: (0, m) if c == 1 else (1, 3 - m))


def moved(array, pairs):
    return lax.ppermute(array, BLOCKS, pairs)


def summed(parts, axes):
    return jnp.sum(lax.all_to_all(parts, axes, 0, 0, tiled=True), axis=0)


def shards(train_acts, train_grads, lengths, query_acts, query_grads, basis_in, basis_out):
    ring = lax.axis_index(RING)
    ring_size = lax.axis_size(RING)
    blocks = lax.axis_size("c") * lax.axis_size("m")
    count = lengths.shape[0]

    other = moved(lengths, OTHER_CORE)
    g00 = rotate_transposed(train_grads, basis_out)
    g00, other, train_acts = lax.optimization_barrier((g00, other, train_acts))
    g10 = moved(g00, GRADS_PARTNER)
    g01 = moved(g00, OTHER_CORE)
    acts = rotate(train_acts, basis_in)
    acts, g01, query_acts, query_grads = lax.optimization_barrier((acts, g01, query_acts, query_grads))
    a1 = moved(acts, ACTS_OTHER)
    a0 = moved(acts, ACTS_SAME)
    core = lax.broadcast_in_dim(lax.axis_index("c"), lengths.shape, ())
    both = jnp.stack([lengths, other, core])

    width, cols = g00.shape[0], a0.shape[1]
    chunk = 2 * width // ring_size
    inner = ring_size // 2
    qa = rotate(query_acts, basis_in)
    qg_own = rotate_transposed(query_grads, basis_out)
    qg_mine = lax.dynamic_slice_in_dim(qg_own, lax.rem(ring, inner) * chunk, chunk, 0)
    g10, qa, qg_mine, both = lax.optimization_barrier((g10, qa, qg_mine, both))
    g11 = moved(g10, OTHER_CORE)
    qa = moved(qa, ACTS_OTHER)
    qg_far = moved(qg_mine, GRADS_PARTNER)
    curvature = curvature_of(ring_size, both, g00, g01, g10, g11, a0, a1)
    curvature, qa, qg_far = lax.optimization_barrier((curvature, qa, qg_far))
    qg = jnp.where(ring < inner, qg_mine, qg_far)
    parts = lax.all_to_all(curvature, RING, 0, 0, tiled=True)
    mine, total = reduced(parts, cols)
    total = total + moved(total, OTHER_CORE)
    total = total + moved(total, GRADS_PARTNER)
    more = moved(total, ACTS_PARTNER)
    scale = 1.0 / (count * lax.axis_size(DP))
    damping_scale = DAMPING_RATIO * scale / (2 * width * cols * blocks)
    mine = precond_of(ring_size, scale, damping_scale, mine, total, more, qg, qa)
    precond = lax.all_to_all(mine, RING, 0, 0, tiled=True).reshape(2 * width, cols)
    found = scores_of(both, precond, g00, g01, g10, g11, a0, a1)
    return summed(found, BLOCKS)[:, 0].reshape(1, count)


def solution(mesh):
    cut = Mesh(np.asarray(mesh.devices).reshape(4, 2, 4, 2, 4), ("x", "zl", "y", "c", "m"))
    return jax.shard_map(
        shards,
        mesh=cut,
        in_specs=(P(DP, None), P(DP, None), P(DP), P(), P(), P(None, "m"), P(None, "m")),
        out_specs=P(None, DP),
        check_vma=False,
    )
```

```python
import functools

import jax
import jax.numpy as jnp
import numpy as np
from jax import lax
from jax.experimental import pallas as pl
from jax.experimental.pallas import tpu as pltpu
from jax.sharding import Mesh
from jax.sharding import PartitionSpec as P

DAMPING_RATIO = 0.1
DP = ("x", "zl", "y", "c")
RING = ("x", "zl", "y")
BLOCKS = ("c", "m")
HALF = 256
LANES = 128
SPARE = 8
VMEM = 16 * 1024 * 1024
f32 = jnp.float32
bf16 = jnp.bfloat16


def params():
    return pltpu.CompilerParams(vmem_limit_bytes=VMEM)


def dot(a, b, contract):
    return lax.dot_general(a, b, (contract, ((), ())), preferred_element_type=f32)


def rotate(values, basis):
    return dot(values, basis, ((1,), (0,))).astype(bf16)


def rotate_transposed(values, basis):
    return dot(basis, values, ((0,), (1,))).astype(bf16)


def in_vmem(*arrays):
    return [pltpu.with_memory_space_constraint(a, pltpu.VMEM) for a in arrays]


def local_call(kernel, shapes, scratch=(), scalars=1):
    def call(*operands):
        here = pl.BlockSpec(memory_space=pltpu.VMEM)
        there = pl.BlockSpec(memory_space=pltpu.SMEM)
        return pl.pallas_call(
            kernel,
            in_specs=[there] * scalars + [here] * (len(operands) - scalars),
            out_specs=[here] * len(shapes),
            out_shape=list(shapes),
            scratch_shapes=list(scratch),
            compiler_params=params(),
        )(*operands[:scalars], *in_vmem(*operands[scalars:]))

    return call


def bounds_of(lengths_ref, which):
    result, at = [], jnp.int32(0)
    for j in range(lengths_ref.shape[1]):
        end = at + lengths_ref[which, j]
        result.append((at, end))
        at = end
    return result


def pick(index, values):
    chosen = values[0]
    for j in range(1, len(values)):
        chosen = jnp.where(index == j, values[j], chosen)
    return chosen


def block_curvature(grads, places, masked, wide, out_ref, first):
    total = None
    for b in range(2):
        product = dot(grads[b][...], wide[b], ((1,), (0,)))
        total = product * product if total is None else total + product * product
    for b, slot, at in places:
        product = dot(grads[b][:, pl.ds(at, HALF)], masked[slot], ((1,), (0,)))
        total = total + product * product
    rows, cols = total.shape
    chunk = (out_ref.shape[1] - SPARE) * LANES // cols
    spare = jnp.zeros((SPARE, LANES), f32)
    for k in range(rows // chunk):
        block = total[k * chunk : (k + 1) * chunk]
        pieces = [block[:, j * LANES : (j + 1) * LANES] for j in range(cols // LANES)]
        out_ref[first + k] = jnp.concatenate([*pieces, spare], axis=0).astype(bf16)
    return jnp.sum(total, axis=0, keepdims=True)


def places_of(lengths_ref):
    count = lengths_ref.shape[1]
    wides, places = [], []
    for b in range(2):
        bounds = bounds_of(lengths_ref, b)
        starts, ends = [v[0] for v in bounds], [v[1] for v in bounds]
        across = jnp.int32(count - 1)
        for j, (start, finish) in enumerate(bounds):
            across = jnp.where((start < HALF) & (finish > HALF), j, across)
        wides.append((pick(across, starts), pick(across, ends)))
        for k in range(count - 1):
            which = k + (k >= across).astype(jnp.int32)
            start = pick(which, starts)
            at = pl.multiple_of(jnp.where(start >= HALF, HALF, 0), HALF)
            places.append((b, b * (count - 1) + k, at, start, pick(which, ends)))
    return wides, places


def curvature_kernel(lengths_ref, g00, g01, g10, g11, a0_ref, a1_ref, out_ref, masked, wide):
    acts = (a0_ref, a1_ref)
    tokens, cols = a0_ref.shape
    row = lax.broadcasted_iota(jnp.int32, (HALF, 1), 0)
    rows = lax.broadcasted_iota(jnp.int32, (tokens, 1), 0)
    wides, places = places_of(lengths_ref)
    for b, (start, finish) in enumerate(wides):
        inside = (rows >= start) & (rows < finish)
        wide[b] = jnp.where(inside, acts[b][...], jnp.zeros((tokens, cols), bf16))
    for b, slot, at, start, finish in places:
        inside = (row + at >= start) & (row + at < finish)
        window = acts[b][pl.ds(at, HALF), :]
        masked[slot] = jnp.where(inside, window, jnp.zeros_like(window))
    places = [p[:3] for p in places]
    sums = block_curvature((g00, g01), places, masked, wide, out_ref, 0)
    sums = sums + block_curvature((g10, g11), places, masked, wide, out_ref, out_ref.shape[0] // 2)
    total = jnp.sum(sums, axis=1, keepdims=True)
    high = total.astype(bf16).astype(f32)
    middle = (total - high).astype(bf16).astype(f32)
    low = total - high - middle
    lane = lax.broadcasted_iota(jnp.int32, (1, LANES), 1)
    terms = jnp.where(lane == 0, high, jnp.where(lane == 1, middle, jnp.where(lane == 2, low, 0.0)))
    terms = jnp.broadcast_to(terms, (SPARE, LANES))
    last = out_ref.shape[1] - 2 * SPARE
    for k in range(out_ref.shape[0]):
        end = out_ref[k, last:, :].astype(f32)
        out_ref[k, last:, :] = jnp.concatenate([end[0:SPARE], terms], axis=0).astype(bf16)


def curvature_of(chunks, lengths, g00, g01, g10, g11, a0, a1):
    width = g00.shape[0]
    tokens, cols = a0.shape
    others = 2 * (lengths.shape[1] - 1)
    shape = (chunks, 2 * width * cols // (chunks * LANES) + SPARE, LANES)
    return local_call(
        curvature_kernel,
        [jax.ShapeDtypeStruct(shape, bf16)],
        [pltpu.VMEM((others, HALF, cols), bf16), pltpu.VMEM((2, tokens, cols), bf16)],
    )(lengths, g00, g01, g10, g11, a0, a1)[0]


def reduce_kernel(parts_ref, chunk_ref, total_ref):
    rows, cols = chunk_ref.shape
    found = parts_ref[0].astype(f32)
    for j in range(1, parts_ref.shape[0]):
        found = found + parts_ref[j].astype(f32)
    pieces = [found[j * rows : (j + 1) * rows] for j in range(cols // LANES)]
    chunk_ref[...] = jnp.concatenate(pieces, axis=1)
    terms = found[found.shape[0] - SPARE :]
    total_ref[...] = jnp.broadcast_to(jnp.sum(terms, axis=1, keepdims=True), total_ref.shape)


def reduced(parts, cols):
    shapes = [((parts.shape[1] - SPARE) * LANES // cols, cols), (SPARE, LANES)]
    return local_call(
        reduce_kernel, [jax.ShapeDtypeStruct(s, f32) for s in shapes], scalars=0
    )(parts)


def precond_kernel(scale, damping_scale, chunk_ref, total_ref, more_ref, qg_ref, qa_ref, out_ref):
    damping = (total_ref[0:1, 0:1] + more_ref[0:1, 0:1]) * damping_scale
    query = dot(qg_ref[...], qa_ref[...], ((1,), (0,)))
    value = (query / (chunk_ref[...] * scale + damping)).astype(bf16)
    for j in range(out_ref.shape[0]):
        out_ref[j] = value


def precond_of(copies, scale, damping_scale, chunk, total, more, qg, qa):
    shape = (copies, *chunk.shape)
    return local_call(
        functools.partial(precond_kernel, scale, damping_scale), [jax.ShapeDtypeStruct(shape, bf16)], scalars=0
    )(chunk, total, more, qg, qa)[0]


def score_kernel(which, lengths_ref, p_ref, near_ref, far_ref, acts_ref, out_ref):
    width, tokens = near_ref.shape
    lane = lax.broadcasted_iota(jnp.int32, (1, tokens), 1)
    sums = jnp.zeros((1, tokens), f32)
    for member, grads in enumerate((near_ref, far_ref)):
        product = dot(p_ref[member * width : (member + 1) * width, :], acts_ref[...], ((1,), (1,)))
        sums = sums + jnp.sum(grads[...].astype(f32) * product, axis=0, keepdims=True)
    for j, (start, finish) in enumerate(bounds_of(lengths_ref, which)):
        inside = (lane >= start) & (lane < finish)
        value = jnp.sum(jnp.where(inside, sums, 0.0), axis=1, keepdims=True)
        out_ref[j : j + 1, :] = jnp.broadcast_to(value, (1, out_ref.shape[1]))


def scores_of(which, lengths, precond, near, far, acts):
    return local_call(
        functools.partial(score_kernel, which), [jax.ShapeDtypeStruct((lengths.shape[1], LANES), f32)]
    )(lengths, precond, near, far, acts)[0]


def routes(f):
    return [(c * 4 + m, f(c, m)[0] * 4 + f(c, m)[1]) for c in range(2) for m in range(4)]


OTHER_CORE = routes(lambda c, m: (1 - c, m))
GRADS_PARTNER = routes(lambda c, m: (c, m ^ 1))
ACTS_PARTNER = routes(lambda c, m: (c, 3 - m))
ACTS_SAME = routes(lambda c, m: (0, m) if c == 0 else (1, 3 - m))
ACTS_OTHER = routes(lambda c, m: (0, m) if c == 1 else (1, 3 - m))


def moved(array, pairs):
    return lax.ppermute(array, BLOCKS, pairs)


def shards(train_acts, train_grads, lengths, query_acts, query_grads, basis_in, basis_out):
    ring = lax.axis_index(RING)
    ring_size = lax.axis_size(RING)
    blocks = lax.axis_size("c") * lax.axis_size("m")
    count = lengths.shape[0]

    other = moved(lengths, OTHER_CORE)
    g00 = rotate_transposed(train_grads, basis_out)
    g00, other, train_acts = lax.optimization_barrier((g00, other, train_acts))
    g10 = moved(g00, GRADS_PARTNER)
    g01 = moved(g00, OTHER_CORE)
    acts = rotate(train_acts, basis_in)
    acts, g01, query_acts, query_grads = lax.optimization_barrier((acts, g01, query_acts, query_grads))
    a1 = moved(acts, ACTS_OTHER)
    a0 = moved(acts, ACTS_SAME)
    both = jnp.stack([lengths, other])

    width, cols = g00.shape[0], a0.shape[1]
    chunk = 2 * width // ring_size
    inner = ring_size // 2
    qa = rotate(query_acts, basis_in)
    qg_own = rotate_transposed(query_grads, basis_out)
    qg_mine = lax.dynamic_slice_in_dim(qg_own, lax.rem(ring, inner) * chunk, chunk, 0)
    g10, qa, qg_mine, both = lax.optimization_barrier((g10, qa, qg_mine, both))
    g11 = moved(g10, OTHER_CORE)
    qa = moved(qa, ACTS_OTHER)
    qg_far = moved(qg_mine, GRADS_PARTNER)
    curvature = curvature_of(ring_size, both, g00, g01, g10, g11, a0, a1)
    curvature, qa, qg_far = lax.optimization_barrier((curvature, qa, qg_far))
    qg = jnp.where(ring < inner, qg_mine, qg_far)
    parts = lax.all_to_all(curvature, RING, 0, 0, tiled=True)
    mine, total = reduced(parts, cols)
    total = total + moved(total, OTHER_CORE)
    total = total + moved(total, GRADS_PARTNER)
    more = moved(total, ACTS_PARTNER)
    scale = 1.0 / (count * lax.axis_size(DP))
    damping_scale = DAMPING_RATIO * scale / (2 * width * cols * blocks)
    mine = precond_of(ring_size, scale, damping_scale, mine, total, more, qg, qa)
    precond = lax.all_to_all(mine, RING, 0, 0, tiled=True).reshape(2 * width, cols)
    found = moved(scores_of(1, both, precond, g01, g11, a1), OTHER_CORE)
    found = found + scores_of(0, both, precond, g00, g10, a0)
    found = found + moved(found, GRADS_PARTNER)
    found = found + moved(found, ACTS_PARTNER)
    return found[:, 0].reshape(1, count)


def solution(mesh):
    cut = Mesh(np.asarray(mesh.devices).reshape(4, 2, 4, 2, 4), ("x", "zl", "y", "c", "m"))
    return jax.shard_map(
        shards,
        mesh=cut,
        in_specs=(P(DP, None), P(DP, None), P(DP), P(), P(), P(None, "m"), P(None, "m")),
        out_specs=P(None, DP),
        check_vma=False,
    )
```

```python
import functools

import jax
import jax.numpy as jnp
import numpy as np
from jax import lax
from jax.experimental import pallas as pl
from jax.experimental.pallas import tpu as pltpu
from jax.sharding import Mesh
from jax.sharding import PartitionSpec as P

DAMPING_RATIO = 0.1
DP = ("x", "zl", "y", "c")
RING = ("x", "zl", "y")
BLOCKS = ("c", "m")
HALF = 256
LANES = 128
SPARE = 8
VMEM = 16 * 1024 * 1024
f32 = jnp.float32
bf16 = jnp.bfloat16


def params():
    return pltpu.CompilerParams(vmem_limit_bytes=VMEM)


def dot(a, b, contract):
    return lax.dot_general(a, b, (contract, ((), ())), preferred_element_type=f32)


def rotate(values, basis):
    return dot(values, basis, ((1,), (0,))).astype(bf16)


def rotate_transposed(values, basis):
    return dot(basis, values, ((0,), (1,))).astype(bf16)


def in_vmem(*arrays):
    return [pltpu.with_memory_space_constraint(a, pltpu.VMEM) for a in arrays]


def local_call(kernel, shapes, scratch=(), scalars=1):
    def call(*operands):
        here = pl.BlockSpec(memory_space=pltpu.VMEM)
        there = pl.BlockSpec(memory_space=pltpu.SMEM)
        return pl.pallas_call(
            kernel,
            in_specs=[there] * scalars + [here] * (len(operands) - scalars),
            out_specs=[here] * len(shapes),
            out_shape=list(shapes),
            scratch_shapes=list(scratch),
            compiler_params=params(),
        )(*operands[:scalars], *in_vmem(*operands[scalars:]))

    return call


def bounds_of(lengths_ref, which):
    result, at = [], jnp.int32(0)
    for j in range(lengths_ref.shape[1]):
        end = at + lengths_ref[which, j]
        result.append((at, end))
        at = end
    return result


def pick(index, values):
    chosen = values[0]
    for j in range(1, len(values)):
        chosen = jnp.where(index == j, values[j], chosen)
    return chosen


def block_curvature(grads, places, masked, wide, out_ref, first):
    total = None
    for b in range(2):
        product = dot(grads[b][...], wide[b], ((1,), (0,)))
        total = product * product if total is None else total + product * product
    for b, slot, at in places:
        product = dot(grads[b][:, pl.ds(at, HALF)], masked[slot], ((1,), (0,)))
        total = total + product * product
    rows, cols = total.shape
    chunk = (out_ref.shape[1] - SPARE) * LANES // cols
    spare = jnp.zeros((SPARE, LANES), f32)
    for k in range(rows // chunk):
        block = total[k * chunk : (k + 1) * chunk]
        pieces = [block[:, j * LANES : (j + 1) * LANES] for j in range(cols // LANES)]
        out_ref[first + k] = jnp.concatenate([*pieces, spare], axis=0).astype(bf16)
    return jnp.sum(total, axis=0, keepdims=True)


def places_of(lengths_ref):
    count = lengths_ref.shape[1]
    wides, places = [], []
    for b in range(2):
        bounds = bounds_of(lengths_ref, b)
        starts, ends = [v[0] for v in bounds], [v[1] for v in bounds]
        across = jnp.int32(count - 1)
        for j, (start, finish) in enumerate(bounds):
            across = jnp.where((start < HALF) & (finish > HALF), j, across)
        wides.append((pick(across, starts), pick(across, ends)))
        for k in range(count - 1):
            which = k + (k >= across).astype(jnp.int32)
            start = pick(which, starts)
            at = pl.multiple_of(jnp.where(start >= HALF, HALF, 0), HALF)
            places.append((b, b * (count - 1) + k, at, start, pick(which, ends)))
    return wides, places


def curvature_kernel(lengths_ref, g00, g01, g10, g11, a0_ref, a1_ref, out_ref, masked, wide):
    acts = (a0_ref, a1_ref)
    tokens, cols = a0_ref.shape
    row = lax.broadcasted_iota(jnp.int32, (HALF, 1), 0)
    rows = lax.broadcasted_iota(jnp.int32, (tokens, 1), 0)
    wides, places = places_of(lengths_ref)
    for b, (start, finish) in enumerate(wides):
        inside = (rows >= start) & (rows < finish)
        wide[b] = jnp.where(inside, acts[b][...], jnp.zeros((tokens, cols), bf16))
    for b, slot, at, start, finish in places:
        inside = (row + at >= start) & (row + at < finish)
        window = acts[b][pl.ds(at, HALF), :]
        masked[slot] = jnp.where(inside, window, jnp.zeros_like(window))
    places = [p[:3] for p in places]
    sums = block_curvature((g00, g01), places, masked, wide, out_ref, 0)
    sums = sums + block_curvature((g10, g11), places, masked, wide, out_ref, out_ref.shape[0] // 2)
    total = jnp.sum(sums, axis=1, keepdims=True)
    high = total.astype(bf16).astype(f32)
    middle = (total - high).astype(bf16).astype(f32)
    low = total - high - middle
    lane = lax.broadcasted_iota(jnp.int32, (1, LANES), 1)
    terms = jnp.where(lane == 0, high, jnp.where(lane == 1, middle, jnp.where(lane == 2, low, 0.0)))
    terms = jnp.broadcast_to(terms, (SPARE, LANES))
    last = out_ref.shape[1] - 2 * SPARE
    for k in range(out_ref.shape[0]):
        end = out_ref[k, last:, :].astype(f32)
        out_ref[k, last:, :] = jnp.concatenate([end[0:SPARE], terms], axis=0).astype(bf16)


def curvature_of(chunks, lengths, g00, g01, g10, g11, a0, a1):
    width = g00.shape[0]
    tokens, cols = a0.shape
    others = 2 * (lengths.shape[1] - 1)
    shape = (chunks, 2 * width * cols // (chunks * LANES) + SPARE, LANES)
    return local_call(
        curvature_kernel,
        [jax.ShapeDtypeStruct(shape, bf16)],
        [pltpu.VMEM((others, HALF, cols), bf16), pltpu.VMEM((2, tokens, cols), bf16)],
    )(lengths, g00, g01, g10, g11, a0, a1)[0]


def reduce_kernel(parts_ref, chunk_ref, total_ref):
    rows, cols = chunk_ref.shape
    found = parts_ref[0].astype(f32)
    for j in range(1, parts_ref.shape[0]):
        found = found + parts_ref[j].astype(f32)
    pieces = [found[j * rows : (j + 1) * rows] for j in range(cols // LANES)]
    chunk_ref[...] = jnp.concatenate(pieces, axis=1)
    terms = found[found.shape[0] - SPARE :]
    total_ref[...] = jnp.broadcast_to(jnp.sum(terms, axis=1, keepdims=True), total_ref.shape)


def reduced(parts, cols):
    shapes = [((parts.shape[1] - SPARE) * LANES // cols, cols), (SPARE, LANES)]
    return local_call(
        reduce_kernel, [jax.ShapeDtypeStruct(s, f32) for s in shapes], scalars=0
    )(parts)


def precond_kernel(scale, damping_scale, chunk_ref, total_ref, more_ref, qg_ref, qa_ref, out_ref):
    damping = (total_ref[0:1, 0:1] + more_ref[0:1, 0:1]) * damping_scale
    query = dot(qg_ref[...], qa_ref[...], ((1,), (0,)))
    value = (query / (chunk_ref[...] * scale + damping)).astype(bf16)
    for j in range(out_ref.shape[0]):
        out_ref[j] = value


def precond_of(copies, scale, damping_scale, chunk, total, more, qg, qa):
    shape = (copies, *chunk.shape)
    return local_call(
        functools.partial(precond_kernel, scale, damping_scale), [jax.ShapeDtypeStruct(shape, bf16)], scalars=0
    )(chunk, total, more, qg, qa)[0]


def score_kernel(which, lengths_ref, p_ref, near_ref, far_ref, acts_ref, out_ref):
    width, tokens = near_ref.shape
    lane = lax.broadcasted_iota(jnp.int32, (1, tokens), 1)
    sums = jnp.zeros((1, tokens), f32)
    for member, grads in enumerate((near_ref, far_ref)):
        product = dot(p_ref[member * width : (member + 1) * width, :], acts_ref[...], ((1,), (1,)))
        sums = sums + jnp.sum(grads[...].astype(f32) * product, axis=0, keepdims=True)
    for j, (start, finish) in enumerate(bounds_of(lengths_ref, which)):
        inside = (lane >= start) & (lane < finish)
        value = jnp.sum(jnp.where(inside, sums, 0.0), axis=1, keepdims=True)
        out_ref[j : j + 1, :] = jnp.broadcast_to(value, (1, out_ref.shape[1]))


def scores_of(which, lengths, precond, near, far, acts):
    return local_call(
        functools.partial(score_kernel, which), [jax.ShapeDtypeStruct((lengths.shape[1], LANES), f32)]
    )(lengths, precond, near, far, acts)[0]


def routes(f):
    return [(c * 4 + m, f(c, m)[0] * 4 + f(c, m)[1]) for c in range(2) for m in range(4)]


OTHER_CORE = routes(lambda c, m: (1 - c, m))
GRADS_PARTNER = routes(lambda c, m: (c, m ^ 1))
ACTS_PARTNER = routes(lambda c, m: (c, 3 - m))
ACTS_SAME = routes(lambda c, m: (0, m) if c == 0 else (1, 3 - m))
ACTS_OTHER = routes(lambda c, m: (0, m) if c == 1 else (1, 3 - m))


def moved(array, pairs):
    return lax.ppermute(array, BLOCKS, pairs)


def shards(train_acts, train_grads, lengths, query_acts, query_grads, basis_in, basis_out):
    ring = lax.axis_index(RING)
    ring_size = lax.axis_size(RING)
    blocks = lax.axis_size("c") * lax.axis_size("m")
    count = lengths.shape[0]

    other = moved(lengths, OTHER_CORE)
    g00 = rotate_transposed(train_grads, basis_out)
    g00, other, train_acts = lax.optimization_barrier((g00, other, train_acts))
    g10 = moved(g00, GRADS_PARTNER)
    g01 = moved(g00, OTHER_CORE)
    acts = rotate(train_acts, basis_in)
    acts, g01, query_acts, query_grads = lax.optimization_barrier((acts, g01, query_acts, query_grads))
    a1 = moved(acts, ACTS_OTHER)
    a0 = moved(acts, ACTS_SAME)
    both = jnp.stack([lengths, other])

    width, cols = g00.shape[0], a0.shape[1]
    chunk = 2 * width // ring_size
    inner = ring_size // 2
    qa = rotate(query_acts, basis_in)
    qg_own = rotate_transposed(query_grads, basis_out)
    qg_mine = lax.dynamic_slice_in_dim(qg_own, lax.rem(ring, inner) * chunk, chunk, 0)
    g10, qa, qg_mine, both = lax.optimization_barrier((g10, qa, qg_mine, both))
    g11 = moved(g10, OTHER_CORE)
    curvature = curvature_of(ring_size, both, g00, g01, g10, g11, a0, a1)
    parts = lax.all_to_all(curvature, RING, 0, 0, tiled=True)
    parts, qa, qg_mine = lax.optimization_barrier((parts, qa, qg_mine))
    qa = moved(qa, ACTS_OTHER)
    qg_far = moved(qg_mine, GRADS_PARTNER)
    qg = jnp.where(ring < inner, qg_mine, qg_far)
    mine, total = reduced(parts, cols)
    total = total + moved(total, OTHER_CORE)
    total = total + moved(total, GRADS_PARTNER)
    more = moved(total, ACTS_PARTNER)
    scale = 1.0 / (count * lax.axis_size(DP))
    damping_scale = DAMPING_RATIO * scale / (2 * width * cols * blocks)
    mine = precond_of(ring_size, scale, damping_scale, mine, total, more, qg, qa)
    precond = lax.all_to_all(mine, RING, 0, 0, tiled=True).reshape(2 * width, cols)
    found = moved(scores_of(1, both, precond, g01, g11, a1), OTHER_CORE)
    found = found + scores_of(0, both, precond, g00, g10, a0)
    found = found + moved(found, GRADS_PARTNER)
    found = found + moved(found, ACTS_PARTNER)
    return found[:, 0].reshape(1, count)


def solution(mesh):
    cut = Mesh(np.asarray(mesh.devices).reshape(4, 2, 4, 2, 4), ("x", "zl", "y", "c", "m"))
    return jax.shard_map(
        shards,
        mesh=cut,
        in_specs=(P(DP, None), P(DP, None), P(DP), P(), P(), P(None, "m"), P(None, "m")),
        out_specs=P(None, DP),
        check_vma=False,
    )
```

```python
import functools

import jax
import jax.numpy as jnp
import numpy as np
from jax import lax
from jax.experimental import pallas as pl
from jax.experimental.pallas import tpu as pltpu
from jax.sharding import Mesh
from jax.sharding import PartitionSpec as P

DAMPING_RATIO = 0.1
DP = ("x", "zl", "y", "c")
RING = ("x", "zl", "y")
BLOCKS = ("c", "m")
HALF = 256
LANES = 128
SPARE = 8
VMEM = 16 * 1024 * 1024
f32 = jnp.float32
bf16 = jnp.bfloat16


def params():
    return pltpu.CompilerParams(vmem_limit_bytes=VMEM)


def dot(a, b, contract):
    return lax.dot_general(a, b, (contract, ((), ())), preferred_element_type=f32)


def rotate(values, basis):
    return dot(values, basis, ((1,), (0,))).astype(bf16)


def rotate_transposed(values, basis):
    return dot(basis, values, ((0,), (1,))).astype(bf16)


def in_vmem(*arrays):
    return [pltpu.with_memory_space_constraint(a, pltpu.VMEM) for a in arrays]


def local_call(kernel, shapes, scratch=(), scalars=1):
    def call(*operands):
        here = pl.BlockSpec(memory_space=pltpu.VMEM)
        there = pl.BlockSpec(memory_space=pltpu.SMEM)
        return pl.pallas_call(
            kernel,
            in_specs=[there] * scalars + [here] * (len(operands) - scalars),
            out_specs=[here] * len(shapes),
            out_shape=list(shapes),
            scratch_shapes=list(scratch),
            compiler_params=params(),
        )(*operands[:scalars], *in_vmem(*operands[scalars:]))

    return call


def bounds_of(lengths_ref, which):
    result, at = [], jnp.int32(0)
    for j in range(lengths_ref.shape[1]):
        end = at + lengths_ref[which, j]
        result.append((at, end))
        at = end
    return result


def pick(index, values):
    chosen = values[0]
    for j in range(1, len(values)):
        chosen = jnp.where(index == j, values[j], chosen)
    return chosen


def block_curvature(grads, places, masked, wide, out_ref, first):
    total = None
    for b in range(2):
        product = dot(grads[b][...], wide[b], ((1,), (0,)))
        total = product * product if total is None else total + product * product
    for b, slot, at in places:
        product = dot(grads[b][:, pl.ds(at, HALF)], masked[slot], ((1,), (0,)))
        total = total + product * product
    rows, cols = total.shape
    chunk = (out_ref.shape[1] - SPARE) * LANES // cols
    spare = jnp.zeros((SPARE, LANES), f32)
    for k in range(rows // chunk):
        block = total[k * chunk : (k + 1) * chunk]
        pieces = [block[:, j * LANES : (j + 1) * LANES] for j in range(cols // LANES)]
        out_ref[first + k] = jnp.concatenate([*pieces, spare], axis=0).astype(bf16)
    return jnp.sum(total, axis=0, keepdims=True)


def places_of(lengths_ref):
    count = lengths_ref.shape[1]
    wides, places = [], []
    for b in range(2):
        bounds = bounds_of(lengths_ref, b)
        starts, ends = [v[0] for v in bounds], [v[1] for v in bounds]
        across = jnp.int32(count - 1)
        for j, (start, finish) in enumerate(bounds):
            across = jnp.where((start < HALF) & (finish > HALF), j, across)
        wides.append((pick(across, starts), pick(across, ends)))
        for k in range(count - 1):
            which = k + (k >= across).astype(jnp.int32)
            start = pick(which, starts)
            at = pl.multiple_of(jnp.where(start >= HALF, HALF, 0), HALF)
            places.append((b, b * (count - 1) + k, at, start, pick(which, ends)))
    return wides, places


def curvature_kernel(lengths_ref, g00, g01, g10, g11, a0_ref, a1_ref, out_ref, masked, wide):
    acts = (a0_ref, a1_ref)
    tokens, cols = a0_ref.shape
    row = lax.broadcasted_iota(jnp.int32, (HALF, 1), 0)
    rows = lax.broadcasted_iota(jnp.int32, (tokens, 1), 0)
    wides, places = places_of(lengths_ref)
    for b, (start, finish) in enumerate(wides):
        inside = (rows >= start) & (rows < finish)
        wide[b] = jnp.where(inside, acts[b][...], jnp.zeros((tokens, cols), bf16))
    for b, slot, at, start, finish in places:
        inside = (row + at >= start) & (row + at < finish)
        window = acts[b][pl.ds(at, HALF), :]
        masked[slot] = jnp.where(inside, window, jnp.zeros_like(window))
    places = [p[:3] for p in places]
    sums = block_curvature((g00, g01), places, masked, wide, out_ref, 0)
    sums = sums + block_curvature((g10, g11), places, masked, wide, out_ref, out_ref.shape[0] // 2)
    total = jnp.sum(sums, axis=1, keepdims=True)
    high = total.astype(bf16).astype(f32)
    middle = (total - high).astype(bf16).astype(f32)
    low = total - high - middle
    lane = lax.broadcasted_iota(jnp.int32, (1, LANES), 1)
    terms = jnp.where(lane == 0, high, jnp.where(lane == 1, middle, jnp.where(lane == 2, low, 0.0)))
    terms = jnp.broadcast_to(terms, (SPARE, LANES))
    last = out_ref.shape[1] - 2 * SPARE
    for k in range(out_ref.shape[0]):
        end = out_ref[k, last:, :].astype(f32)
        out_ref[k, last:, :] = jnp.concatenate([end[0:SPARE], terms], axis=0).astype(bf16)


def curvature_of(chunks, lengths, g00, g01, g10, g11, a0, a1):
    width = g00.shape[0]
    tokens, cols = a0.shape
    others = 2 * (lengths.shape[1] - 1)
    shape = (chunks, 2 * width * cols // (chunks * LANES) + SPARE, LANES)
    return local_call(
        curvature_kernel,
        [jax.ShapeDtypeStruct(shape, bf16)],
        [pltpu.VMEM((others, HALF, cols), bf16), pltpu.VMEM((2, tokens, cols), bf16)],
    )(lengths, g00, g01, g10, g11, a0, a1)[0]


def reduce_kernel(parts_ref, chunk_ref, total_ref):
    rows, cols = chunk_ref.shape
    found = parts_ref[0].astype(f32)
    for j in range(1, parts_ref.shape[0]):
        found = found + parts_ref[j].astype(f32)
    pieces = [found[j * rows : (j + 1) * rows] for j in range(cols // LANES)]
    chunk_ref[...] = jnp.concatenate(pieces, axis=1)
    terms = found[found.shape[0] - SPARE :]
    total_ref[...] = jnp.broadcast_to(jnp.sum(terms, axis=1, keepdims=True), total_ref.shape)


def reduced(parts, cols):
    shapes = [((parts.shape[1] - SPARE) * LANES // cols, cols), (SPARE, LANES)]
    return local_call(
        reduce_kernel, [jax.ShapeDtypeStruct(s, f32) for s in shapes], scalars=0
    )(parts)


def precond_kernel(scale, damping_scale, chunk_ref, total_ref, more_ref, qg_ref, qa_ref, out_ref):
    damping = (total_ref[0:1, 0:1] + more_ref[0:1, 0:1]) * damping_scale
    query = dot(qg_ref[...], qa_ref[...], ((1,), (0,)))
    value = (query / (chunk_ref[...] * scale + damping)).astype(bf16)
    for j in range(out_ref.shape[0]):
        out_ref[j] = value


def precond_of(copies, scale, damping_scale, chunk, total, more, qg, qa):
    shape = (copies, *chunk.shape)
    return local_call(
        functools.partial(precond_kernel, scale, damping_scale), [jax.ShapeDtypeStruct(shape, bf16)], scalars=0
    )(chunk, total, more, qg, qa)[0]


def score_kernel(which, lengths_ref, p_ref, near_ref, far_ref, acts_ref, out_ref):
    width, tokens = near_ref.shape
    lane = lax.broadcasted_iota(jnp.int32, (1, tokens), 1)
    sums = jnp.zeros((1, tokens), f32)
    for member, grads in enumerate((near_ref, far_ref)):
        product = dot(p_ref[member * width : (member + 1) * width, :], acts_ref[...], ((1,), (1,)))
        sums = sums + jnp.sum(grads[...].astype(f32) * product, axis=0, keepdims=True)
    place = lax.broadcasted_iota(jnp.int32, out_ref.shape, 1)
    found = jnp.zeros(out_ref.shape, f32)
    for j, (start, finish) in enumerate(bounds_of(lengths_ref, which)):
        inside = (lane >= start) & (lane < finish)
        value = jnp.sum(jnp.where(inside, sums, 0.0), axis=1, keepdims=True)
        found = jnp.where(place == j, value, found)
    out_ref[...] = found


def scores_of(which, lengths, precond, near, far, acts):
    return local_call(
        functools.partial(score_kernel, which), [jax.ShapeDtypeStruct((1, LANES), f32)]
    )(lengths, precond, near, far, acts)[0]


def routes(f):
    return [(c * 4 + m, f(c, m)[0] * 4 + f(c, m)[1]) for c in range(2) for m in range(4)]


OTHER_CORE = routes(lambda c, m: (1 - c, m))
GRADS_PARTNER = routes(lambda c, m: (c, m ^ 1))
ACTS_PARTNER = routes(lambda c, m: (c, 3 - m))
ACTS_SAME = routes(lambda c, m: (0, m) if c == 0 else (1, 3 - m))
ACTS_OTHER = routes(lambda c, m: (0, m) if c == 1 else (1, 3 - m))


def moved(array, pairs):
    return lax.ppermute(array, BLOCKS, pairs)


def shards(train_acts, train_grads, lengths, query_acts, query_grads, basis_in, basis_out):
    ring = lax.axis_index(RING)
    ring_size = lax.axis_size(RING)
    blocks = lax.axis_size("c") * lax.axis_size("m")
    count = lengths.shape[0]

    other = moved(lengths, OTHER_CORE)
    g00 = rotate_transposed(train_grads, basis_out)
    g00, other, train_acts = lax.optimization_barrier((g00, other, train_acts))
    g10 = moved(g00, GRADS_PARTNER)
    g01 = moved(g00, OTHER_CORE)
    acts = rotate(train_acts, basis_in)
    acts, g01, query_acts, query_grads = lax.optimization_barrier((acts, g01, query_acts, query_grads))
    a1 = moved(acts, ACTS_OTHER)
    a0 = moved(acts, ACTS_SAME)
    both = jnp.stack([lengths, other])

    width, cols = g00.shape[0], a0.shape[1]
    chunk = 2 * width // ring_size
    inner = ring_size // 2
    qa = rotate(query_acts, basis_in)
    qg_own = rotate_transposed(query_grads, basis_out)
    qg_mine = lax.dynamic_slice_in_dim(qg_own, lax.rem(ring, inner) * chunk, chunk, 0)
    g10, qa, qg_mine, both = lax.optimization_barrier((g10, qa, qg_mine, both))
    g11 = moved(g10, OTHER_CORE)
    qa = moved(qa, ACTS_OTHER)
    qg_far = moved(qg_mine, GRADS_PARTNER)
    curvature = curvature_of(ring_size, both, g00, g01, g10, g11, a0, a1)
    curvature, qa, qg_far = lax.optimization_barrier((curvature, qa, qg_far))
    qg = jnp.where(ring < inner, qg_mine, qg_far)
    parts = lax.all_to_all(curvature, RING, 0, 0, tiled=True)
    mine, total = reduced(parts, cols)
    total = total + moved(total, OTHER_CORE)
    total = total + moved(total, GRADS_PARTNER)
    more = moved(total, ACTS_PARTNER)
    scale = 1.0 / (count * lax.axis_size(DP))
    damping_scale = DAMPING_RATIO * scale / (2 * width * cols * blocks)
    mine = precond_of(ring_size, scale, damping_scale, mine, total, more, qg, qa)
    precond = lax.all_to_all(mine, RING, 0, 0, tiled=True).reshape(2 * width, cols)
    found = moved(scores_of(1, both, precond, g01, g11, a1), OTHER_CORE)
    found = found + scores_of(0, both, precond, g00, g10, a0)
    found = found + moved(found, GRADS_PARTNER)
    found = found + moved(found, ACTS_PARTNER)
    return found[:, 0:count]


def solution(mesh):
    cut = Mesh(np.asarray(mesh.devices).reshape(4, 2, 4, 2, 4), ("x", "zl", "y", "c", "m"))
    return jax.shard_map(
        shards,
        mesh=cut,
        in_specs=(P(DP, None), P(DP, None), P(DP), P(), P(), P(None, "m"), P(None, "m")),
        out_specs=P(None, DP),
        check_vma=False,
    )
```
